32 devices in a mesh: lon: 8 (over z, x), lat: 4 (over y, core).
Axes of the slice: x: 2, y: 2, z: 4, core: 2. Of those that a mesh axis runs over, the one named last changes fastest.
Arguments:
- fields: float32 [6, 4, 512, 1024], P(None, None, 'lat', 'lon'), may hold values from -6 to 6
- face_weights: float32 [2, 512, 1024], P(None, 'lat', 'lon'), may hold values from 0.5 to 1.5
- inv_area: float32 [512, 1024], P('lat', 'lon'), may hold values from 0.5 to 1.5
- cell_mask: int32 [512, 1024], P('lat', 'lon'), may hold values 0 or 1
- land_blocks: int32 [4, 8], P('lat', 'lon'), may hold values 0 or 1
Outputs:
- new_fields: float32 [6, 4, 512, 1024], P(None, None, 'lat', 'lon')
The draws below stay inside these ranges and needn't reach their ends.
All inputs are finite; a program needn't handle non-finite values. No bound on the sum of `cell_mask` or of `land_blocks` on one device may be relied on, other than what follows from the above.
Results may differ from the reference program's by a relative error of at most 0.00002.
Values sent between devices are 32-bit elements; how exact they have to be, the bound alone decides.
A program may use at most 64 MiB of HBM per device.

```python
import jax
import jax.numpy as jnp

CI = 128
CJ = 128
NF = 6
NK = 4
SUBSTEPS = 2
NI = 1024
NJ = 512
BLOCKS_LAT = 4
BLOCKS_LON = 8


def touch_ends(entries, key, smallest, high):
    extent = entries.shape
    spot = [jax.random.randint(jax.random.fold_in(key, axis), (), 0, extent[axis]) for axis in range(len(extent))]
    entries = entries.at[tuple(spot)].set(smallest)
    longest = extent.index(max(extent))
    spot[longest] = (spot[longest] + 1) % extent[longest]
    return entries.at[tuple(spot)].set(high)


def block_levels(stream_key, dims, pieces, least, largest):
    level = 1.0
    for dim, shards_of in pieces:
        heights = jax.random.uniform(jax.random.fold_in(jax.random.fold_in(stream_key, 6), dim), (shards_of,), jnp.float32, least / len(pieces), largest / len(pieces))
        level = level * jnp.repeat(jnp.exp(heights), dims[dim] // shards_of).reshape((-1,) + (1,) * (len(dims) - 1 - dim))
    return level


def gaussian(own_key, dims, width, most, split=(), dtype=jnp.bfloat16):
    drawn = width * jax.random.normal(own_key, dims, jnp.float32)
    if split:
        drawn = drawn * block_levels(own_key, dims, split, -0.22, 0.18)
    return jnp.clip(drawn, -most, most).astype(dtype)


def setup_inputs(seed: int = 0) -> dict:
    arg_keys = jax.random.split(jax.random.key(seed), 6)
    return {
        "fields": gaussian(arg_keys[0], (NF, NK, NJ, NI), 1.0, 6.0, ((2, 4), (3, 8)), jnp.float32),
        "face_weights": jnp.clip(0.5 + 1.0 * jax.random.uniform(arg_keys[1], (2, NJ, NI), jnp.float32) ** block_levels(arg_keys[1], (2, NJ, NI), ((1, 4), (2, 8)), -0.2, 0.2), 0.5, 1.5),
        "inv_area": jnp.clip(0.5 + 1.0 * jax.random.uniform(arg_keys[2], (NJ, NI), jnp.float32) ** block_levels(arg_keys[2], (NJ, NI), ((0, 4), (1, 8)), -0.2, 0.2), 0.5, 1.5),
        "cell_mask": touch_ends((jax.random.randint(arg_keys[3], (NJ, NI), 0, 5) < 4).astype(jnp.int32), jax.random.fold_in(arg_keys[3], 1), 0, 1),
        "land_blocks": touch_ends((jax.random.randint(arg_keys[4], (BLOCKS_LAT, BLOCKS_LON), 0, 4) < 1).astype(jnp.int32), jax.random.fold_in(arg_keys[4], 1), 0, 1),
    }


TIME_STEP = 0.1
ADVECTION = 0.5


def face_flux(near_side, far_side, face_speed, face_weight):
    return face_weight * (ADVECTION * face_speed * (near_side + far_side) * 0.5 - (far_side - near_side))


def tendency(lon_fields, lat_fields, east_ext, north_ext, inv_area):
    u_speed = lon_fields[4]
    east_speed = 0.5 * (u_speed[..., :-1] + u_speed[..., 1:])
    flux_east = face_flux(lon_fields[..., :-1], lon_fields[..., 1:], east_speed, east_ext)
    v_speed = lat_fields[5]
    north_speed = 0.5 * (v_speed[:, :-1, :] + v_speed[:, 1:, :])
    flux_north = face_flux(lat_fields[:, :, :-1, :], lat_fields[:, :, 1:, :], north_speed, north_ext)
    return inv_area * ((flux_east[..., :-1] - flux_east[..., 1:]) + (flux_north[:, :, :-1, :] - flux_north[:, :, 1:, :]))


def reference(fields, face_weights, inv_area, cell_mask, land_blocks):
    land_cells = jnp.repeat(jnp.repeat(land_blocks, CJ, axis=0), CI, axis=1)
    ocean_mask = cell_mask.astype(jnp.float32) * (1 - land_cells).astype(jnp.float32)
    flip_sign = jnp.where(jnp.arange(NF) >= 4, -1.0, 1.0).astype(jnp.float32)[:, None, None]
    east_weight = face_weights[0]
    north_weight = face_weights[1]
    east_ext = jnp.concatenate([east_weight[:, -1:], east_weight], axis=1)
    north_ext = jnp.concatenate([jnp.zeros_like(north_weight[:1]), north_weight], axis=0)
    current = fields
    for substep in range(SUBSTEPS):
        lon_fields = jnp.concatenate([current[..., -1:], current, current[..., :1]], axis=-1)
        fold_row = current[:, :, -1, ::-1] * flip_sign
        south_zero = jnp.zeros_like(current[:, :, :1, :])
        lat_fields = jnp.concatenate([south_zero, current, fold_row[:, :, None, :]], axis=2)
        change = tendency(lon_fields, lat_fields, east_ext, north_ext, inv_area)
        current = current + TIME_STEP * ocean_mask * change
    return current
```

```python
import jax
import jax.numpy as jnp
from jax import lax
from jax.experimental import pallas as pl
from jax.experimental.pallas import tpu as pltpu
from jax.sharding import PartitionSpec as P

TIME_STEP = 0.1
PAD = 8
CHUNK = 32
LANES = 128
WEST, EAST, SOUTH, NORTH, SOUTHWEST, SOUTHEAST, NORTHWEST, NORTHEAST = range(8)


def lanes_of(shape):
    return lax.broadcasted_iota(jnp.int32, shape, len(shape) - 1)


def rows_of(shape):
    return lax.broadcasted_iota(jnp.int32, shape, len(shape) - 2)


def roll(value, shift, axis):
    return pltpu.roll(value, shift % value.shape[axis], axis)


def take_lanes(value, index):
    return jnp.take_along_axis(value, index, axis=1)


def stencil(c, x, left, right, south, north):
    c0, ce, cw, cn, cs = c
    return c0 * x + ce * right + cw * left + cn * north + cs * south


def coefficients(base, ke, kw, kn, ks, u, u_left, u_right, v, v_south, v_north):
    pe = ke * (0.125 * (u + u_right))
    pw = kw * (0.125 * (u + u_left))
    pn = kn * (0.125 * (v + v_north))
    ps = ks * (0.125 * (v + v_south))
    return base + ((pw - pe) + (ps - pn)), ke - pe, kw + pw, kn - pn, ks + ps


def kernel(
    nlon, nlat, nfield, nlevel,
    fields, face_weights, inv_area, cell_mask, land,
    out,
    ext0, ext1, obuf, weights, area, cells, scale, packed, send_s, send_n,
    recv_we, recv_ns, recv_c, halo0, halo1, coef, strips, nrows, srows, edge_rows,
    in_sems, out_sems, send_sems, recv_sems,
):
    nplane = nfield * nlevel
    rows = ext0.shape[1] - 2 * PAD
    top_row, low_row = PAD + rows, PAD - 1
    lon, lat = lax.axis_index("lon"), lax.axis_index("lat")
    is_top = lat == nlat - 1
    is_bottom = lat == 0
    east, west = lax.rem(lon + 1, nlon), lax.rem(lon + nlon - 1, nlon)
    north_lat = jnp.where(is_top, lat, lat + 1)
    north_lon = jnp.where(is_top, nlon - 1 - lon, lon)
    ne_lon = jnp.where(is_top, lax.rem(2 * nlon - 2 - lon, nlon), east)
    nw_lon = jnp.where(is_top, lax.rem(nlon - lon, nlon), west)
    ne_self = jnp.logical_and(is_top, ne_lon == lon)
    nw_self = jnp.logical_and(is_top, nw_lon == lon)
    ne_other = jnp.logical_not(ne_self)
    nw_other = jnp.logical_not(nw_self)
    not_bottom = jnp.logical_not(is_bottom)

    barrier = pltpu.get_barrier_semaphore()

    def greet(to_lon, to_lat):
        pl.semaphore_signal(
            barrier, inc=1, device_id={"lon": to_lon, "lat": to_lat},
            device_id_type=pl.DeviceIdType.MESH,
        )

    greet(west, lat)
    greet(east, lat)
    greet(north_lon, north_lat)

    @pl.when(ne_other)
    def _():
        greet(ne_lon, north_lat)

    @pl.when(nw_other)
    def _():
        greet(nw_lon, north_lat)

    @pl.when(not_bottom)
    def _():
        greet(lon, lat - 1)
        greet(east, lat - 1)
        greet(west, lat - 1)

    loads = [
        pltpu.make_async_copy(fields, ext0.at[:, pl.ds(PAD, rows), :], in_sems.at[0]),
        pltpu.make_async_copy(face_weights, weights, in_sems.at[1]),
        pltpu.make_async_copy(inv_area, area, in_sems.at[2]),
        pltpu.make_async_copy(cell_mask, cells, in_sems.at[3]),
    ]
    for load in loads:
        load.start()
    for load in loads[1:]:
        load.wait()
    sea = (1 - land[0, 0]).astype(jnp.float32)
    scale[...] = (TIME_STEP * sea) * cells[...].astype(jnp.float32) * area[...]
    loads[0].wait()

    group = lanes_of((CHUNK, LANES)) // 4
    for start in range(0, rows, CHUNK):
        piece = pl.ds(start, CHUNK)
        gathered = jnp.zeros((CHUNK, LANES), jnp.float32)
        for p in range(nplane + 3):
            if p < nplane:
                plane = ext0[p, pl.ds(PAD + start, CHUNK), :]
            elif p < nplane + 2:
                plane = weights[p - nplane, piece, :]
            else:
                plane = scale[piece, :]
            gathered = jnp.where(group == p, roll(plane, 4 * p + 2, 1), gathered)
        packed[piece, :] = gathered
    for buf, first, second, corner in ((send_s, 0, 1, 0), (send_n, rows - 1, rows - 2, rows - 8)):
        for at, row in ((0, first), (32, second)):
            for p in range(nplane):
                buf[pl.ds(at + p, 1), :] = ext0[p, pl.ds(PAD + row, 1), :]
            for i in range(2):
                buf[pl.ds(at + nplane + i, 1), :] = weights[i, pl.ds(row, 1), :]
            buf[pl.ds(at + nplane + 2, 1), :] = scale[pl.ds(row, 1), :]
            buf[pl.ds(at + nplane + 3, 5), :] = jnp.zeros((5, LANES), jnp.float32)
        buf[pl.ds(64, 8), :] = packed[pl.ds(corner, 8), :]

    def remote(src, dst, number, slot, to_lon, to_lat):
        return pltpu.make_async_remote_copy(
            src_ref=src, dst_ref=dst, send_sem=send_sems.at[number], recv_sem=recv_sems.at[slot],
            device_id={"lon": to_lon, "lat": to_lat}, device_id_type=pl.DeviceIdType.MESH,
        )

    corner_s, corner_n = send_s.at[pl.ds(64, 8), :], send_n.at[pl.ds(64, 8), :]
    go_w = remote(packed, recv_we.at[1], 0, EAST, west, lat)
    go_e = remote(packed, recv_we.at[0], 1, WEST, east, lat)
    go_n = remote(
        send_n, recv_ns.at[jnp.where(is_top, 1, 0)], 2,
        jnp.where(is_top, NORTH, SOUTH), north_lon, north_lat,
    )
    go_ne = remote(
        corner_n, recv_c.at[jnp.where(is_top, 3, 0)], 3,
        jnp.where(is_top, NORTHEAST, SOUTHWEST), ne_lon, north_lat,
    )
    go_nw = remote(
        corner_n, recv_c.at[jnp.where(is_top, 2, 1)], 4,
        jnp.where(is_top, NORTHWEST, SOUTHEAST), nw_lon, north_lat,
    )
    go_s = remote(send_s, recv_ns.at[1], 5, NORTH, lon, lat - 1)
    go_se = remote(corner_s, recv_c.at[2], 6, NORTHWEST, east, lat - 1)
    go_sw = remote(corner_s, recv_c.at[3], 7, NORTHEAST, west, lat - 1)

    greetings = 3 + jnp.where(ne_self, 0, 1) + jnp.where(nw_self, 0, 1) + jnp.where(is_bottom, 0, 3)
    pl.semaphore_wait(barrier, greetings)
    go_w.start()
    go_e.start()
    go_n.start()

    @pl.when(ne_other)
    def _():
        go_ne.start()

    @pl.when(nw_other)
    def _():
        go_nw.start()

    @pl.when(not_bottom)
    def _():
        go_s.start()
        go_se.start()
        go_sw.start()

    @pl.when(ne_self)
    def _():
        recv_c[3] = send_n[pl.ds(64, 8), :]

    @pl.when(nw_self)
    def _():
        recv_c[2] = send_n[pl.ds(64, 8), :]

    @pl.when(is_bottom)
    def _():
        recv_ns[0] = jnp.zeros(recv_ns.shape[1:], jnp.float32)
        recv_c[0] = jnp.zeros(recv_c.shape[1:], jnp.float32)
        recv_c[1] = jnp.zeros(recv_c.shape[1:], jnp.float32)

    def arrived(dst, slot):
        remote(dst, dst, 0, slot, west, lat).wait_recv()

    arrived(recv_we.at[0], WEST)
    arrived(recv_we.at[1], EAST)
    arrived(recv_ns.at[1], NORTH)

    @pl.when(not_bottom)
    def _():
        arrived(recv_ns.at[0], SOUTH)
        arrived(recv_c.at[0], SOUTHWEST)
        arrived(recv_c.at[1], SOUTHEAST)

    @pl.when(ne_other)
    def _():
        arrived(recv_c.at[3], NORTHEAST)

    @pl.when(nw_other)
    def _():
        arrived(recv_c.at[2], NORTHWEST)

    go_w.wait_send()
    go_e.wait_send()
    go_n.wait_send()

    @pl.when(ne_other)
    def _():
        go_ne.wait_send()

    @pl.when(nw_other)
    def _():
        go_nw.wait_send()

    @pl.when(not_bottom)
    def _():
        go_s.wait_send()
        go_se.wait_send()
        go_sw.wait_send()

    def at_top(shape):
        return jnp.full(shape, lat, jnp.int32) == nlat - 1

    shape = (64, LANES)
    came = recv_ns[1, pl.ds(0, 64), :]
    sub = rows_of(shape) % 32
    flips = jnp.where(jnp.logical_and(sub >= 4 * nlevel, sub < nplane), -1.0, 1.0)
    nrows[...] = jnp.where(
        at_top(shape), flips * take_lanes(came, LANES - 1 - lanes_of(shape)), came
    )
    srows[...] = recv_ns[0, pl.ds(0, 64), :]
    for p in range(nplane):
        ext0[p, pl.ds(top_row, 1), :] = nrows[pl.ds(p, 1), :]
        ext0[p, pl.ds(low_row, 1), :] = srows[pl.ds(p, 1), :]

    eight = (8, LANES)
    lane8 = lanes_of(eight)
    slot8 = lane8 % 4
    flip8 = jnp.where(jnp.logical_and(lane8 >= 16 * nlevel, lane8 < 4 * nplane), -1.0, 1.0)
    east8 = lane8 // 4 == nplane

    def beyond(block):
        upside = jnp.concatenate([block[7 - i : 8 - i, :] for i in range(8)], axis=0)
        mirrored = flip8 * take_lanes(upside, lane8 - slot8 + (3 - slot8))
        mirrored = jnp.where(east8, roll(mirrored, -1, 1), mirrored)
        return mirrored

    middle_n = recv_ns[1, pl.ds(64, 8), :]
    middle_s = recv_ns[0, pl.ds(64, 8), :]
    slot = lanes_of((rows, LANES)) % 4
    strips[0, pl.ds(PAD, rows), :] = jnp.where(slot < 2, recv_we[0], packed[...])
    strips[1, pl.ds(PAD, rows), :] = jnp.where(slot < 2, packed[...], recv_we[1])
    strips[0, pl.ds(0, 8), :] = jnp.where(slot8 < 2, recv_c[0], middle_s)
    strips[1, pl.ds(0, 8), :] = jnp.where(slot8 < 2, middle_s, recv_c[1])
    for side in range(2):
        lower, upper = ((recv_c[2], middle_n), (middle_n, recv_c[3]))[side]
        strips[side, pl.ds(top_row, 8), :] = jnp.where(
            at_top(eight),
            beyond(jnp.where(slot8 >= 2, lower, upper)),
            jnp.where(slot8 < 2, lower, upper),
        )

    tall = (rows + 2 * PAD, LANES)
    slot_t = lanes_of(tall) % 4
    lane_t = lanes_of(tall)
    folded = jnp.logical_and(at_top(tall), rows_of(tall) == top_row)

    def halo_of(west_strip, east_strip):
        return jnp.where(slot_t == 1, west_strip, roll(east_strip, -2, 1))

    advanced = []
    for side in range(2):
        x = strips[side]
        u = take_lanes(x, 16 * nlevel + lane_t % (4 * nlevel))
        v = take_lanes(x, 20 * nlevel + lane_t % (4 * nlevel))
        e_weight, n_weight, k = (
            take_lanes(x, 4 * (nplane + i) + slot_t) for i in range(3)
        )
        n_behind = roll(n_weight, 1, 0)
        n_south = jnp.where(folded, n_weight, n_behind)
        n_north = jnp.where(folded, roll(n_weight, -1, 0), n_weight)
        ke, kw, kn, ks = k * e_weight, k * roll(e_weight, 1, 1), k * n_north, k * n_south
        base = 1.0 - ((ke + kw) + (kn + ks))
        c = coefficients(
            base, ke, kw, kn, ks,
            u, roll(u, 1, 1), roll(u, -1, 1), v, roll(v, 1, 0), roll(v, -1, 0),
        )
        advanced.append(
            stencil(c, x, roll(x, 1, 1), roll(x, -1, 1), roll(x, 1, 0), roll(x, -1, 0))
        )
    halo0[...] = halo_of(strips[0], strips[1])
    halo1[...] = halo_of(advanced[0], advanced[1])

    lane_c = lanes_of((CHUNK, LANES))
    for start in range(0, rows, CHUNK):
        piece = pl.ds(start, CHUNK)
        k = scale[piece, :]
        e_weight = weights[0, piece, :]
        n_weight = weights[1, piece, :]
        outer = roll(strips[0, pl.ds(PAD + start, CHUNK), :], -(4 * nplane + 1), 1)
        w_weight = jnp.where(lane_c == 0, outer, roll(e_weight, 1, 1))
        if start:
            s_weight = weights[1, pl.ds(start - 1, CHUNK), :]
        else:
            s_weight = jnp.where(
                rows_of((CHUNK, LANES)) == 0, srows[pl.ds(nplane + 1, 1), :], roll(n_weight, 1, 0)
            )
        ke, kw, kn, ks = k * e_weight, k * w_weight, k * n_weight, k * s_weight
        coef[0, piece, :] = 1.0 - ((ke + kw) + (kn + ks))
        coef[1, piece, :] = ke
        coef[2, piece, :] = kw
        coef[3, piece, :] = kn
        coef[4, piece, :] = ks

    flat = (nplane, LANES)
    lane_f = lanes_of(flat)
    plane_f = rows_of(flat)

    def spread(value):
        return jnp.concatenate([value] * nfield, axis=0)

    for which, buf, row, inner in ((0, srows, low_row, PAD), (1, nrows, top_row, top_row - 1)):
        for p in range(nplane):
            edge_rows[pl.ds(p, 1), :] = ext0[p, pl.ds(inner, 1), :]
        x, outer, within = buf[pl.ds(0, nplane), :], buf[pl.ds(32, nplane), :], edge_rows[...]
        south, north = (outer, within) if which == 0 else (within, outer)
        ends = jnp.broadcast_to(halo0[pl.ds(row, 1), :], flat)
        at_west = jnp.sum(jnp.where(lane_f == 4 * plane_f + 1, ends, 0.0), axis=1, keepdims=True)
        at_east = jnp.sum(jnp.where(lane_f == 4 * plane_f, ends, 0.0), axis=1, keepdims=True)
        left = jnp.where(lane_f == 0, at_west, roll(x, 1, 1))
        right = jnp.where(lane_f == LANES - 1, at_east, roll(x, -1, 1))
        raw = buf[pl.ds(nplane, 1), :]
        n_near = buf[pl.ds(nplane + 1, 1), :]
        n_far = buf[pl.ds(32 + nplane + 1, 1), :]
        k = buf[pl.ds(nplane + 2, 1), :]
        one = (1, LANES)
        lane_1 = lanes_of(one)
        w_end = roll(strips[0, pl.ds(row, 1), :], -(4 * nplane + 1), 1)
        e_end = roll(strips[1, pl.ds(row, 1), :], LANES - 1 - (4 * nplane + 1), 1)
        if which == 1:
            shifted = roll(raw, -1, 1)
            e_weight = jnp.where(at_top(one), shifted, raw)
        else:
            e_weight = raw
        e_weight = jnp.where(lane_1 == LANES - 1, e_end, e_weight)
        w_weight = jnp.where(lane_1 == 0, w_end, roll(e_weight, 1, 1))
        if which == 0:
            n_north, n_south = n_near, n_far
        else:
            n_north = jnp.where(at_top(one), n_far, n_near)
            n_south = jnp.where(at_top(one), n_near, weights[1, pl.ds(rows - 1, 1), :])
        ke, kw, kn, ks = k * e_weight, k * w_weight, k * n_north, k * n_south
        base = 1.0 - ((ke + kw) + (kn + ks))
        at_u, at_v = slice(4 * nlevel, 5 * nlevel), slice(5 * nlevel, 6 * nlevel)
        c = coefficients(
            base, ke, kw, kn, ks,
            spread(x[at_u]), spread(left[at_u]), spread(right[at_u]),
            spread(x[at_v]), spread(south[at_v]), spread(north[at_v]),
        )
        edge_rows[...] = stencil(c, x, left, right, south, north)
        for p in range(nplane):
            ext1[p, pl.ds(row, 1), :] = edge_rows[pl.ds(p, 1), :]

    def advance(source, halo, level, put):
        for start in range(0, rows, CHUNK):
            piece = pl.ds(start, CHUNK)
            base, ke, kw, kn, ks = (coef[i, piece, :] for i in range(5))
            ends = halo[pl.ds(PAD + start, CHUNK), :]

            def centre(field):
                return source[field * nlevel + level, pl.ds(PAD + start, CHUNK), :]

            def sides(field, x):
                end = pltpu.roll(ends, LANES - 1 - 4 * (field * nlevel + level), 1)
                return (
                    jnp.where(lane_c == 0, end, roll(x, 1, 1)),
                    jnp.where(lane_c == LANES - 1, end, roll(x, -1, 1)),
                )

            def rows_beside(field):
                return (
                    source[field * nlevel + level, pl.ds(PAD + start - 1, CHUNK), :],
                    source[field * nlevel + level, pl.ds(PAD + start + 1, CHUNK), :],
                )

            u, v = centre(4), centre(5)
            u_sides, v_sides = sides(4, u), rows_beside(5)
            c = coefficients(base, ke, kw, kn, ks, u, *u_sides, v, *v_sides)
            for field in range(nfield):
                x = centre(field)
                left, right = u_sides if field == 4 else sides(field, x)
                south, north = v_sides if field == 5 else rows_beside(field)
                put(field, start, stencil(c, x, left, right, south, north))

    @pl.loop(0, nlevel)
    def _(level):
        def put(field, start, value):
            ext1[field * nlevel + level, pl.ds(PAD + start, CHUNK), :] = value

        advance(ext0, halo0, level, put)

    def store(level):
        return pltpu.make_async_copy(obuf.at[level], out.at[:, level], out_sems.at[level])

    @pl.loop(0, nlevel)
    def _(level):
        def put(field, start, value):
            obuf[level, field, pl.ds(start, CHUNK), :] = value

        advance(ext1, halo1, level, put)
        store(level).start()

    for level in range(nlevel):
        store(level).wait()


def solution(mesh):
    nlon, nlat = mesh.shape["lon"], mesh.shape["lat"]

    def local(fields, face_weights, inv_area, cell_mask, land_blocks):
        nfield, nlevel, rows, cols = fields.shape
        nplane = nfield * nlevel
        tall = rows + 2 * PAD
        f32 = jnp.float32
        anywhere = pl.BlockSpec(memory_space=pl.ANY)

        def body(*refs):
            kernel(nlon, nlat, nfield, nlevel, *refs)

        return pl.pallas_call(
            body,
            out_shape=jax.ShapeDtypeStruct(fields.shape, f32),
            in_specs=[anywhere] * 4 + [pl.BlockSpec(memory_space=pltpu.SMEM)],
            out_specs=anywhere,
            scratch_shapes=[
                pltpu.VMEM((nplane, tall, cols), f32),
                pltpu.VMEM((nplane, tall, cols), f32),
                pltpu.VMEM((nlevel, nfield, rows, cols), f32),
                pltpu.VMEM((2, rows, cols), f32),
                pltpu.VMEM((rows, cols), f32),
                pltpu.VMEM((rows, cols), jnp.int32),
                pltpu.VMEM((rows, cols), f32),
                pltpu.VMEM((rows, cols), f32),
                pltpu.VMEM((72, cols), f32),
                pltpu.VMEM((72, cols), f32),
                pltpu.VMEM((2, rows, cols), f32),
                pltpu.VMEM((2, 72, cols), f32),
                pltpu.VMEM((4, 8, cols), f32),
                pltpu.VMEM((tall, cols), f32),
                pltpu.VMEM((tall, cols), f32),
                pltpu.VMEM((5, rows, cols), f32),
                pltpu.VMEM((2, tall, cols), f32),
                pltpu.VMEM((64, cols), f32),
                pltpu.VMEM((64, cols), f32),
                pltpu.VMEM((nplane, cols), f32),
                pltpu.SemaphoreType.DMA((4,)),
                pltpu.SemaphoreType.DMA((nlevel,)),
                pltpu.SemaphoreType.DMA((8,)),
                pltpu.SemaphoreType.DMA((8,)),
            ],
            compiler_params=pltpu.CompilerParams(
                collective_id=0, has_side_effects=True, vmem_limit_bytes=32 * 1024 * 1024
            ),
        )(fields.reshape(nplane, rows, cols), face_weights, inv_area, cell_mask, land_blocks)

    in_specs = (
        P(None, None, "lat", "lon"),
        P(None, "lat", "lon"),
        P("lat", "lon"),
        P("lat", "lon"),
        P("lat", "lon"),
    )
    out_specs = P(None, None, "lat", "lon")
    return jax.shard_map(local, mesh=mesh, in_specs=in_specs, out_specs=out_specs, check_vma=False)
```

```python
import jax
import jax.numpy as jnp
from jax import lax
from jax.experimental import pallas as pl
from jax.experimental.pallas import tpu as pltpu
from jax.sharding import PartitionSpec as P

TIME_STEP = 0.1
PAD = 8
CHUNK = 32
LANES = 128
WEST, EAST, SOUTH, NORTH, SOUTHWEST, SOUTHEAST, NORTHWEST, NORTHEAST = range(8)


def lanes_of(shape):
    return lax.broadcasted_iota(jnp.int32, shape, len(shape) - 1)


def rows_of(shape):
    return lax.broadcasted_iota(jnp.int32, shape, len(shape) - 2)


def roll(value, shift, axis):
    return pltpu.roll(value, shift % value.shape[axis], axis)


def take_lanes(value, index):
    return jnp.take_along_axis(value, index, axis=1)


def stencil(c, x, left, right, south, north):
    c0, ce, cw, cn, cs = c
    return c0 * x + ce * right + cw * left + cn * north + cs * south


def coefficients(base, ke, kw, kn, ks, u, u_left, u_right, v, v_south, v_north):
    pe = ke * (0.125 * (u + u_right))
    pw = kw * (0.125 * (u + u_left))
    pn = kn * (0.125 * (v + v_north))
    ps = ks * (0.125 * (v + v_south))
    return base + ((pw - pe) + (ps - pn)), ke - pe, kw + pw, kn - pn, ks + ps


def advance(source, halo, coef, nfield, nlevel, level, put):
    rows = coef.shape[1]
    lane_c = lanes_of((CHUNK, LANES))
    for start in range(0, rows, CHUNK):
        piece = pl.ds(start, CHUNK)
        base, ke, kw, kn, ks = (coef[i, piece, :] for i in range(5))
        ends = halo[pl.ds(PAD + start, CHUNK), :]

        def centre(field):
            return source[field * nlevel + level, pl.ds(PAD + start, CHUNK), :]

        def sides(field, x):
            end = pltpu.roll(ends, LANES - 1 - 4 * (field * nlevel + level), 1)
            return (
                jnp.where(lane_c == 0, end, roll(x, 1, 1)),
                jnp.where(lane_c == LANES - 1, end, roll(x, -1, 1)),
            )

        def rows_beside(field):
            return (
                source[field * nlevel + level, pl.ds(PAD + start - 1, CHUNK), :],
                source[field * nlevel + level, pl.ds(PAD + start + 1, CHUNK), :],
            )

        u, v = centre(4), centre(5)
        u_sides, v_sides = sides(4, u), rows_beside(5)
        c = coefficients(base, ke, kw, kn, ks, u, *u_sides, v, *v_sides)
        for field in range(nfield):
            x = centre(field)
            left, right = u_sides if field == 4 else sides(field, x)
            south, north = v_sides if field == 5 else rows_beside(field)
            put(field, start, stencil(c, x, left, right, south, north))


def first_kernel(
    nlon, nlat, nfield, nlevel,
    fields, face_weights, inv_area, cell_mask, land,
    ext1, halo1, coef,
    ext0, weights, area, cells, scale, packed, send_s, send_n,
    recv_we, recv_ns, recv_c, halo0, strips, nrows, srows, edge_rows,
    in_sems, send_sems, recv_sems,
):
    nplane = nfield * nlevel
    rows = ext0.shape[1] - 2 * PAD
    top_row, low_row = PAD + rows, PAD - 1
    lon, lat = lax.axis_index("lon"), lax.axis_index("lat")
    is_top = lat == nlat - 1
    is_bottom = lat == 0
    east, west = lax.rem(lon + 1, nlon), lax.rem(lon + nlon - 1, nlon)
    north_lat = jnp.where(is_top, lat, lat + 1)
    north_lon = jnp.where(is_top, nlon - 1 - lon, lon)
    ne_lon = jnp.where(is_top, lax.rem(2 * nlon - 2 - lon, nlon), east)
    nw_lon = jnp.where(is_top, lax.rem(nlon - lon, nlon), west)
    ne_self = jnp.logical_and(is_top, ne_lon == lon)
    nw_self = jnp.logical_and(is_top, nw_lon == lon)
    ne_other = jnp.logical_not(ne_self)
    nw_other = jnp.logical_not(nw_self)
    not_bottom = jnp.logical_not(is_bottom)

    barrier = pltpu.get_barrier_semaphore()

    def greet(to_lon, to_lat):
        pl.semaphore_signal(
            barrier, inc=1, device_id={"lon": to_lon, "lat": to_lat},
            device_id_type=pl.DeviceIdType.MESH,
        )

    greet(west, lat)
    greet(east, lat)
    greet(north_lon, north_lat)

    @pl.when(ne_other)
    def _():
        greet(ne_lon, north_lat)

    @pl.when(nw_other)
    def _():
        greet(nw_lon, north_lat)

    @pl.when(not_bottom)
    def _():
        greet(lon, lat - 1)
        greet(east, lat - 1)
        greet(west, lat - 1)

    loads = [
        pltpu.make_async_copy(fields, ext0.at[:, pl.ds(PAD, rows), :], in_sems.at[0]),
        pltpu.make_async_copy(face_weights, weights, in_sems.at[1]),
        pltpu.make_async_copy(inv_area, area, in_sems.at[2]),
        pltpu.make_async_copy(cell_mask, cells, in_sems.at[3]),
    ]
    for load in loads:
        load.start()
    for load in loads[1:]:
        load.wait()
    sea = (1 - land[0, 0]).astype(jnp.float32)
    scale[...] = (TIME_STEP * sea) * cells[...].astype(jnp.float32) * area[...]
    loads[0].wait()

    group = lanes_of((CHUNK, LANES)) // 4
    for start in range(0, rows, CHUNK):
        piece = pl.ds(start, CHUNK)
        gathered = jnp.zeros((CHUNK, LANES), jnp.float32)
        for p in range(nplane + 3):
            if p < nplane:
                plane = ext0[p, pl.ds(PAD + start, CHUNK), :]
            elif p < nplane + 2:
                plane = weights[p - nplane, piece, :]
            else:
                plane = scale[piece, :]
            gathered = jnp.where(group == p, roll(plane, 4 * p + 2, 1), gathered)
        packed[piece, :] = gathered
    for buf, first, second, corner in ((send_s, 0, 1, 0), (send_n, rows - 1, rows - 2, rows - 8)):
        for at, row in ((0, first), (32, second)):
            for p in range(nplane):
                buf[pl.ds(at + p, 1), :] = ext0[p, pl.ds(PAD + row, 1), :]
            for i in range(2):
                buf[pl.ds(at + nplane + i, 1), :] = weights[i, pl.ds(row, 1), :]
            buf[pl.ds(at + nplane + 2, 1), :] = scale[pl.ds(row, 1), :]
            buf[pl.ds(at + nplane + 3, 5), :] = jnp.zeros((5, LANES), jnp.float32)
        buf[pl.ds(64, 8), :] = packed[pl.ds(corner, 8), :]

    def remote(src, dst, number, slot, to_lon, to_lat):
        return pltpu.make_async_remote_copy(
            src_ref=src, dst_ref=dst, send_sem=send_sems.at[number], recv_sem=recv_sems.at[slot],
            device_id={"lon": to_lon, "lat": to_lat}, device_id_type=pl.DeviceIdType.MESH,
        )

    corner_s, corner_n = send_s.at[pl.ds(64, 8), :], send_n.at[pl.ds(64, 8), :]
    go_w = remote(packed, recv_we.at[1], 0, EAST, west, lat)
    go_e = remote(packed, recv_we.at[0], 1, WEST, east, lat)
    go_n = remote(
        send_n, recv_ns.at[jnp.where(is_top, 1, 0)], 2,
        jnp.where(is_top, NORTH, SOUTH), north_lon, north_lat,
    )
    go_ne = remote(
        corner_n, recv_c.at[jnp.where(is_top, 3, 0)], 3,
        jnp.where(is_top, NORTHEAST, SOUTHWEST), ne_lon, north_lat,
    )
    go_nw = remote(
        corner_n, recv_c.at[jnp.where(is_top, 2, 1)], 4,
        jnp.where(is_top, NORTHWEST, SOUTHEAST), nw_lon, north_lat,
    )
    go_s = remote(send_s, recv_ns.at[1], 5, NORTH, lon, lat - 1)
    go_se = remote(corner_s, recv_c.at[2], 6, NORTHWEST, east, lat - 1)
    go_sw = remote(corner_s, recv_c.at[3], 7, NORTHEAST, west, lat - 1)

    greetings = 3 + jnp.where(ne_self, 0, 1) + jnp.where(nw_self, 0, 1) + jnp.where(is_bottom, 0, 3)
    pl.semaphore_wait(barrier, greetings)
    go_w.start()
    go_e.start()
    go_n.start()

    @pl.when(ne_other)
    def _():
        go_ne.start()

    @pl.when(nw_other)
    def _():
        go_nw.start()

    @pl.when(not_bottom)
    def _():
        go_s.start()
        go_se.start()
        go_sw.start()

    @pl.when(ne_self)
    def _():
        recv_c[3] = send_n[pl.ds(64, 8), :]

    @pl.when(nw_self)
    def _():
        recv_c[2] = send_n[pl.ds(64, 8), :]

    @pl.when(is_bottom)
    def _():
        recv_ns[0] = jnp.zeros(recv_ns.shape[1:], jnp.float32)
        recv_c[0] = jnp.zeros(recv_c.shape[1:], jnp.float32)
        recv_c[1] = jnp.zeros(recv_c.shape[1:], jnp.float32)

    def arrived(dst, slot):
        remote(dst, dst, 0, slot, west, lat).wait_recv()

    arrived(recv_we.at[0], WEST)
    arrived(recv_we.at[1], EAST)
    arrived(recv_ns.at[1], NORTH)

    @pl.when(not_bottom)
    def _():
        arrived(recv_ns.at[0], SOUTH)
        arrived(recv_c.at[0], SOUTHWEST)
        arrived(recv_c.at[1], SOUTHEAST)

    @pl.when(ne_other)
    def _():
        arrived(recv_c.at[3], NORTHEAST)

    @pl.when(nw_other)
    def _():
        arrived(recv_c.at[2], NORTHWEST)

    go_w.wait_send()
    go_e.wait_send()
    go_n.wait_send()

    @pl.when(ne_other)
    def _():
        go_ne.wait_send()

    @pl.when(nw_other)
    def _():
        go_nw.wait_send()

    @pl.when(not_bottom)
    def _():
        go_s.wait_send()
        go_se.wait_send()
        go_sw.wait_send()

    def at_top(shape):
        return jnp.full(shape, lat, jnp.int32) == nlat - 1

    shape = (64, LANES)
    came = recv_ns[1, pl.ds(0, 64), :]
    sub = rows_of(shape) % 32
    flips = jnp.where(jnp.logical_and(sub >= 4 * nlevel, sub < nplane), -1.0, 1.0)
    nrows[...] = jnp.where(
        at_top(shape), flips * take_lanes(came, LANES - 1 - lanes_of(shape)), came
    )
    srows[...] = recv_ns[0, pl.ds(0, 64), :]
    for p in range(nplane):
        ext0[p, pl.ds(top_row, 1), :] = nrows[pl.ds(p, 1), :]
        ext0[p, pl.ds(low_row, 1), :] = srows[pl.ds(p, 1), :]

    eight = (8, LANES)
    lane8 = lanes_of(eight)
    slot8 = lane8 % 4
    flip8 = jnp.where(jnp.logical_and(lane8 >= 16 * nlevel, lane8 < 4 * nplane), -1.0, 1.0)
    east8 = lane8 // 4 == nplane

    def beyond(block):
        upside = jnp.concatenate([block[7 - i : 8 - i, :] for i in range(8)], axis=0)
        mirrored = flip8 * take_lanes(upside, lane8 - slot8 + (3 - slot8))
        mirrored = jnp.where(east8, roll(mirrored, -1, 1), mirrored)
        return mirrored

    middle_n = recv_ns[1, pl.ds(64, 8), :]
    middle_s = recv_ns[0, pl.ds(64, 8), :]
    slot = lanes_of((rows, LANES)) % 4
    strips[0, pl.ds(PAD, rows), :] = jnp.where(slot < 2, recv_we[0], packed[...])
    strips[1, pl.ds(PAD, rows), :] = jnp.where(slot < 2, packed[...], recv_we[1])
    strips[0, pl.ds(0, 8), :] = jnp.where(slot8 < 2, recv_c[0], middle_s)
    strips[1, pl.ds(0, 8), :] = jnp.where(slot8 < 2, middle_s, recv_c[1])
    for side in range(2):
        lower, upper = ((recv_c[2], middle_n), (middle_n, recv_c[3]))[side]
        strips[side, pl.ds(top_row, 8), :] = jnp.where(
            at_top(eight),
            beyond(jnp.where(slot8 >= 2, lower, upper)),
            jnp.where(slot8 < 2, lower, upper),
        )

    tall = (rows + 2 * PAD, LANES)
    slot_t = lanes_of(tall) % 4
    lane_t = lanes_of(tall)
    folded = jnp.logical_and(at_top(tall), rows_of(tall) == top_row)

    def halo_of(west_strip, east_strip):
        return jnp.where(slot_t == 1, west_strip, roll(east_strip, -2, 1))

    advanced = []
    for side in range(2):
        x = strips[side]
        u = take_lanes(x, 16 * nlevel + lane_t % (4 * nlevel))
        v = take_lanes(x, 20 * nlevel + lane_t % (4 * nlevel))
        e_weight, n_weight, k = (
            take_lanes(x, 4 * (nplane + i) + slot_t) for i in range(3)
        )
        n_behind = roll(n_weight, 1, 0)
        n_south = jnp.where(folded, n_weight, n_behind)
        n_north = jnp.where(folded, roll(n_weight, -1, 0), n_weight)
        ke, kw, kn, ks = k * e_weight, k * roll(e_weight, 1, 1), k * n_north, k * n_south
        base = 1.0 - ((ke + kw) + (kn + ks))
        c = coefficients(
            base, ke, kw, kn, ks,
            u, roll(u, 1, 1), roll(u, -1, 1), v, roll(v, 1, 0), roll(v, -1, 0),
        )
        advanced.append(
            stencil(c, x, roll(x, 1, 1), roll(x, -1, 1), roll(x, 1, 0), roll(x, -1, 0))
        )
    halo0[...] = halo_of(strips[0], strips[1])
    halo1[...] = halo_of(advanced[0], advanced[1])

    lane_c = lanes_of((CHUNK, LANES))
    for start in range(0, rows, CHUNK):
        piece = pl.ds(start, CHUNK)
        k = scale[piece, :]
        e_weight = weights[0, piece, :]
        n_weight = weights[1, piece, :]
        outer = roll(strips[0, pl.ds(PAD + start, CHUNK), :], -(4 * nplane + 1), 1)
        w_weight = jnp.where(lane_c == 0, outer, roll(e_weight, 1, 1))
        if start:
            s_weight = weights[1, pl.ds(start - 1, CHUNK), :]
        else:
            s_weight = jnp.where(
                rows_of((CHUNK, LANES)) == 0, srows[pl.ds(nplane + 1, 1), :], roll(n_weight, 1, 0)
            )
        ke, kw, kn, ks = k * e_weight, k * w_weight, k * n_weight, k * s_weight
        coef[0, piece, :] = 1.0 - ((ke + kw) + (kn + ks))
        coef[1, piece, :] = ke
        coef[2, piece, :] = kw
        coef[3, piece, :] = kn
        coef[4, piece, :] = ks

    flat = (nplane, LANES)
    lane_f = lanes_of(flat)
    plane_f = rows_of(flat)

    def spread(value):
        return jnp.concatenate([value] * nfield, axis=0)

    for which, buf, row, inner in ((0, srows, low_row, PAD), (1, nrows, top_row, top_row - 1)):
        for p in range(nplane):
            edge_rows[pl.ds(p, 1), :] = ext0[p, pl.ds(inner, 1), :]
        x, outer, within = buf[pl.ds(0, nplane), :], buf[pl.ds(32, nplane), :], edge_rows[...]
        south, north = (outer, within) if which == 0 else (within, outer)
        ends = jnp.broadcast_to(halo0[pl.ds(row, 1), :], flat)
        at_west = jnp.sum(jnp.where(lane_f == 4 * plane_f + 1, ends, 0.0), axis=1, keepdims=True)
        at_east = jnp.sum(jnp.where(lane_f == 4 * plane_f, ends, 0.0), axis=1, keepdims=True)
        left = jnp.where(lane_f == 0, at_west, roll(x, 1, 1))
        right = jnp.where(lane_f == LANES - 1, at_east, roll(x, -1, 1))
        raw = buf[pl.ds(nplane, 1), :]
        n_near = buf[pl.ds(nplane + 1, 1), :]
        n_far = buf[pl.ds(32 + nplane + 1, 1), :]
        k = buf[pl.ds(nplane + 2, 1), :]
        one = (1, LANES)
        lane_1 = lanes_of(one)
        w_end = roll(strips[0, pl.ds(row, 1), :], -(4 * nplane + 1), 1)
        e_end = roll(strips[1, pl.ds(row, 1), :], LANES - 1 - (4 * nplane + 1), 1)
        if which == 1:
            shifted = roll(raw, -1, 1)
            e_weight = jnp.where(at_top(one), shifted, raw)
        else:
            e_weight = raw
        e_weight = jnp.where(lane_1 == LANES - 1, e_end, e_weight)
        w_weight = jnp.where(lane_1 == 0, w_end, roll(e_weight, 1, 1))
        if which == 0:
            n_north, n_south = n_near, n_far
        else:
            n_north = jnp.where(at_top(one), n_far, n_near)
            n_south = jnp.where(at_top(one), n_near, weights[1, pl.ds(rows - 1, 1), :])
        ke, kw, kn, ks = k * e_weight, k * w_weight, k * n_north, k * n_south
        base = 1.0 - ((ke + kw) + (kn + ks))
        at_u, at_v = slice(4 * nlevel, 5 * nlevel), slice(5 * nlevel, 6 * nlevel)
        c = coefficients(
            base, ke, kw, kn, ks,
            spread(x[at_u]), spread(left[at_u]), spread(right[at_u]),
            spread(x[at_v]), spread(south[at_v]), spread(north[at_v]),
        )
        edge_rows[...] = stencil(c, x, left, right, south, north)
        for p in range(nplane):
            ext1[p, pl.ds(row, 1), :] = edge_rows[pl.ds(p, 1), :]

    @pl.loop(0, nlevel)
    def _(level):
        def put(field, start, value):
            ext1[field * nlevel + level, pl.ds(PAD + start, CHUNK), :] = value

        advance(ext0, halo0, coef, nfield, nlevel, level, put)


def second_kernel(nfield, nlevel, ext1, halo1, coef, out, obuf, out_sems):
    def store(level):
        return pltpu.make_async_copy(obuf.at[level], out.at[:, level], out_sems.at[level])

    @pl.loop(0, nlevel)
    def _(level):
        def put(field, start, value):
            obuf[level, field, pl.ds(start, CHUNK), :] = value

        advance(ext1, halo1, coef, nfield, nlevel, level, put)
        store(level).start()

    for level in range(nlevel):
        store(level).wait()


def solution(mesh):
    nlon, nlat = mesh.shape["lon"], mesh.shape["lat"]

    def local(fields, face_weights, inv_area, cell_mask, land_blocks):
        nfield, nlevel, rows, cols = fields.shape
        nplane = nfield * nlevel
        tall = rows + 2 * PAD
        f32 = jnp.float32
        anywhere = pl.BlockSpec(memory_space=pl.ANY)
        near = pl.BlockSpec(memory_space=pltpu.VMEM)

        def far(value):
            return pltpu.with_memory_space_constraint(value, pltpu.HBM)

        def first(*refs):
            first_kernel(nlon, nlat, nfield, nlevel, *refs)

        def second(*refs):
            second_kernel(nfield, nlevel, *refs)

        passed = pl.pallas_call(
            first,
            out_shape=[
                pltpu.VMEM((nplane, tall, cols), f32),
                pltpu.VMEM((tall, cols), f32),
                pltpu.VMEM((5, rows, cols), f32),
            ],
            in_specs=[anywhere] * 4 + [pl.BlockSpec(memory_space=pltpu.SMEM)],
            out_specs=[near] * 3,
            scratch_shapes=[
                pltpu.VMEM((nplane, tall, cols), f32),
                pltpu.VMEM((2, rows, cols), f32),
                pltpu.VMEM((rows, cols), f32),
                pltpu.VMEM((rows, cols), jnp.int32),
                pltpu.VMEM((rows, cols), f32),
                pltpu.VMEM((rows, cols), f32),
                pltpu.VMEM((72, cols), f32),
                pltpu.VMEM((72, cols), f32),
                pltpu.VMEM((2, rows, cols), f32),
                pltpu.VMEM((2, 72, cols), f32),
                pltpu.VMEM((4, 8, cols), f32),
                pltpu.VMEM((tall, cols), f32),
                pltpu.VMEM((2, tall, cols), f32),
                pltpu.VMEM((64, cols), f32),
                pltpu.VMEM((64, cols), f32),
                pltpu.VMEM((nplane, cols), f32),
                pltpu.SemaphoreType.DMA((4,)),
                pltpu.SemaphoreType.DMA((8,)),
                pltpu.SemaphoreType.DMA((8,)),
            ],
            compiler_params=pltpu.CompilerParams(
                collective_id=0, has_side_effects=True, vmem_limit_bytes=16 * 1024 * 1024
            ),
        )(
            far(fields.reshape(nplane, rows, cols)), far(face_weights), far(inv_area),
            far(cell_mask), land_blocks,
        )
        return pl.pallas_call(
            second,
            out_shape=pltpu.HBM(fields.shape, f32),
            in_specs=[near] * 3,
            out_specs=anywhere,
            scratch_shapes=[
                pltpu.VMEM((nlevel, nfield, rows, cols), f32),
                pltpu.SemaphoreType.DMA((nlevel,)),
            ],
            compiler_params=pltpu.CompilerParams(vmem_limit_bytes=16 * 1024 * 1024),
        )(*(pltpu.with_memory_space_constraint(value, pltpu.VMEM) for value in passed))

    in_specs = (
        P(None, None, "lat", "lon"),
        P(None, "lat", "lon"),
        P("lat", "lon"),
        P("lat", "lon"),
        P("lat", "lon"),
    )
    out_specs = P(None, None, "lat", "lon")
    return jax.shard_map(local, mesh=mesh, in_specs=in_specs, out_specs=out_specs, check_vma=False)
```

```python
import jax
import jax.numpy as jnp
from jax import lax
from jax.experimental import pallas as pl
from jax.experimental.pallas import tpu as pltpu
from jax.sharding import PartitionSpec as P

TIME_STEP = 0.1
PAD = 8
CHUNK = 32
LANES = 128
WEST, EAST, SOUTH, NORTH, SOUTHWEST, SOUTHEAST, NORTHWEST, NORTHEAST = range(8)


def lanes_of(shape):
    return lax.broadcasted_iota(jnp.int32, shape, len(shape) - 1)


def rows_of(shape):
    return lax.broadcasted_iota(jnp.int32, shape, len(shape) - 2)


def roll(value, shift, axis):
    return pltpu.roll(value, shift % value.shape[axis], axis)


def take_lanes(value, index):
    return jnp.take_along_axis(value, index, axis=1)


def stencil(c, x, left, right, south, north):
    c0, ce, cw, cn, cs = c
    return c0 * x + ce * right + cw * left + cn * north + cs * south


def coefficients(base, ke, kw, kn, ks, u, u_left, u_right, v, v_south, v_north):
    pe = ke * (0.125 * (u + u_right))
    pw = kw * (0.125 * (u + u_left))
    pn = kn * (0.125 * (v + v_north))
    ps = ks * (0.125 * (v + v_south))
    return base + ((pw - pe) + (ps - pn)), ke - pe, kw + pw, kn - pn, ks + ps


def advance(source, halo, coef, nfield, nlevel, level, put):
    rows = coef.shape[1]
    lane_c = lanes_of((CHUNK, LANES))
    for start in range(0, rows, CHUNK):
        piece = pl.ds(start, CHUNK)
        base, ke, kw, kn, ks = (coef[i, piece, :] for i in range(5))
        ends = None if halo is None else halo[pl.ds(PAD + start, CHUNK), :]

        def centre(field):
            return source[field * nlevel + level, pl.ds(PAD + start, CHUNK), :]

        def sides(field, x):
            if ends is None:
                return roll(x, 1, 1), roll(x, -1, 1)
            end = pltpu.roll(ends, LANES - 1 - 4 * (field * nlevel + level), 1)
            return (
                jnp.where(lane_c == 0, end, roll(x, 1, 1)),
                jnp.where(lane_c == LANES - 1, end, roll(x, -1, 1)),
            )

        def rows_beside(field):
            return (
                source[field * nlevel + level, pl.ds(PAD + start - 1, CHUNK), :],
                source[field * nlevel + level, pl.ds(PAD + start + 1, CHUNK), :],
            )

        u, v = centre(4), centre(5)
        u_sides, v_sides = sides(4, u), rows_beside(5)
        c = coefficients(base, ke, kw, kn, ks, u, *u_sides, v, *v_sides)
        for field in range(nfield):
            x = centre(field)
            left, right = u_sides if field == 4 else sides(field, x)
            south, north = v_sides if field == 5 else rows_beside(field)
            put(field, start, stencil(c, x, left, right, south, north))


def first_kernel(
    nlon, nlat, nfield, nlevel,
    fields, face_weights, inv_area, cell_mask, land,
    ext1, halo1, coef,
    ext0, weights, area, cells, scale, packed, send_s, send_n,
    send_we, recv_we, recv_ns, recv_c, edges, strips, nrows, srows, edge_rows,
    in_sems, send_sems, recv_sems,
):
    nplane = nfield * nlevel
    rows = ext0.shape[1] - 2 * PAD
    top_row, low_row = PAD + rows, PAD - 1
    lon, lat = lax.axis_index("lon"), lax.axis_index("lat")
    is_top = lat == nlat - 1
    is_bottom = lat == 0
    east, west = lax.rem(lon + 1, nlon), lax.rem(lon + nlon - 1, nlon)
    north_lat = jnp.where(is_top, lat, lat + 1)
    north_lon = jnp.where(is_top, nlon - 1 - lon, lon)
    ne_lon = jnp.where(is_top, lax.rem(2 * nlon - 2 - lon, nlon), east)
    nw_lon = jnp.where(is_top, lax.rem(nlon - lon, nlon), west)
    ne_self = jnp.logical_and(is_top, ne_lon == lon)
    nw_self = jnp.logical_and(is_top, nw_lon == lon)
    ne_other = jnp.logical_not(ne_self)
    nw_other = jnp.logical_not(nw_self)
    not_bottom = jnp.logical_not(is_bottom)

    barrier = pltpu.get_barrier_semaphore()

    def greet(to_lon, to_lat):
        pl.semaphore_signal(
            barrier, inc=1, device_id={"lon": to_lon, "lat": to_lat},
            device_id_type=pl.DeviceIdType.MESH,
        )

    greet(west, lat)
    greet(east, lat)
    greet(north_lon, north_lat)

    @pl.when(ne_other)
    def _():
        greet(ne_lon, north_lat)

    @pl.when(nw_other)
    def _():
        greet(nw_lon, north_lat)

    @pl.when(not_bottom)
    def _():
        greet(lon, lat - 1)
        greet(east, lat - 1)
        greet(west, lat - 1)

    starts = range(0, rows, CHUNK)
    loads = [
        pltpu.make_async_copy(face_weights, weights, in_sems.at[0]),
        pltpu.make_async_copy(inv_area, area, in_sems.at[1]),
        pltpu.make_async_copy(cell_mask, cells, in_sems.at[2]),
    ]
    pieces = [
        pltpu.make_async_copy(
            fields.at[:, pl.ds(start, CHUNK), :], ext0.at[:, pl.ds(PAD + start, CHUNK), :],
            in_sems.at[3 + i],
        )
        for i, start in enumerate(starts)
    ]
    for load in loads + pieces:
        load.start()
    for load in loads:
        load.wait()
    sea = (1 - land[0, 0]).astype(jnp.float32)
    scale[...] = (TIME_STEP * sea) * cells[...].astype(jnp.float32) * area[...]

    group = lanes_of((CHUNK, LANES)) // 4
    for start, load in zip(starts, pieces):
        piece = pl.ds(start, CHUNK)
        load.wait()
        gathered = jnp.zeros((CHUNK, LANES), jnp.float32)
        for p in range(nplane + 3):
            if p < nplane:
                plane = ext0[p, pl.ds(PAD + start, CHUNK), :]
            elif p < nplane + 2:
                plane = weights[p - nplane, piece, :]
            else:
                plane = scale[piece, :]
            gathered = jnp.where(group == p, roll(plane, 4 * p + 2, 1), gathered)
        packed[piece, :] = gathered
    half = rows // 2
    lane_h = lanes_of((half, LANES))
    pick = 4 * ((lane_h % 64) // 2) + lane_h % 2
    for side in range(2):
        send_we[side] = jnp.where(
            lane_h < 64,
            take_lanes(packed[pl.ds(0, half), :], pick + 2 * side),
            take_lanes(packed[pl.ds(half, half), :], pick + 2 * side),
        )
    for buf, first, second, corner in ((send_s, 0, 1, 0), (send_n, rows - 1, rows - 2, rows - 8)):
        for at, row in ((0, first), (32, second)):
            for p in range(nplane):
                buf[pl.ds(at + p, 1), :] = ext0[p, pl.ds(PAD + row, 1), :]
            for i in range(2):
                buf[pl.ds(at + nplane + i, 1), :] = weights[i, pl.ds(row, 1), :]
            buf[pl.ds(at + nplane + 2, 1), :] = scale[pl.ds(row, 1), :]
            buf[pl.ds(at + nplane + 3, 5), :] = jnp.zeros((5, LANES), jnp.float32)
        buf[pl.ds(64, 8), :] = packed[pl.ds(corner, 8), :]

    def remote(src, dst, number, slot, to_lon, to_lat):
        return pltpu.make_async_remote_copy(
            src_ref=src, dst_ref=dst, send_sem=send_sems.at[number], recv_sem=recv_sems.at[slot],
            device_id={"lon": to_lon, "lat": to_lat}, device_id_type=pl.DeviceIdType.MESH,
        )

    corner_s, corner_n = send_s.at[pl.ds(64, 8), :], send_n.at[pl.ds(64, 8), :]
    go_w = remote(send_we.at[1], recv_we.at[1], 0, EAST, west, lat)
    go_e = remote(send_we.at[0], recv_we.at[0], 1, WEST, east, lat)
    go_n = remote(
        send_n, recv_ns.at[jnp.where(is_top, 1, 0)], 2,
        jnp.where(is_top, NORTH, SOUTH), north_lon, north_lat,
    )
    go_ne = remote(
        corner_n, recv_c.at[jnp.where(is_top, 3, 0)], 3,
        jnp.where(is_top, NORTHEAST, SOUTHWEST), ne_lon, north_lat,
    )
    go_nw = remote(
        corner_n, recv_c.at[jnp.where(is_top, 2, 1)], 4,
        jnp.where(is_top, NORTHWEST, SOUTHEAST), nw_lon, north_lat,
    )
    go_s = remote(send_s, recv_ns.at[1], 5, NORTH, lon, lat - 1)
    go_se = remote(corner_s, recv_c.at[2], 6, NORTHWEST, east, lat - 1)
    go_sw = remote(corner_s, recv_c.at[3], 7, NORTHEAST, west, lat - 1)

    greetings = 3 + jnp.where(ne_self, 0, 1) + jnp.where(nw_self, 0, 1) + jnp.where(is_bottom, 0, 3)
    pl.semaphore_wait(barrier, greetings)
    go_w.start()
    go_e.start()
    go_n.start()

    @pl.when(ne_other)
    def _():
        go_ne.start()

    @pl.when(nw_other)
    def _():
        go_nw.start()

    @pl.when(not_bottom)
    def _():
        go_s.start()
        go_se.start()
        go_sw.start()

    @pl.when(ne_self)
    def _():
        recv_c[3] = send_n[pl.ds(64, 8), :]

    @pl.when(nw_self)
    def _():
        recv_c[2] = send_n[pl.ds(64, 8), :]

    @pl.when(is_bottom)
    def _():
        recv_ns[0] = jnp.zeros(recv_ns.shape[1:], jnp.float32)
        recv_c[0] = jnp.zeros(recv_c.shape[1:], jnp.float32)
        recv_c[1] = jnp.zeros(recv_c.shape[1:], jnp.float32)

    def set_coefficients(complete):
        lane_c = lanes_of((CHUNK, LANES))
        for start in starts:
            piece = pl.ds(start, CHUNK)
            k = scale[piece, :]
            e_weight = weights[0, piece, :]
            n_weight = weights[1, piece, :]
            w_weight = roll(e_weight, 1, 1)
            if complete:
                outer = roll(strips[0, pl.ds(PAD + start, CHUNK), :], -(4 * nplane + 1), 1)
                w_weight = jnp.where(lane_c == 0, outer, w_weight)
            if start:
                s_weight = weights[1, pl.ds(start - 1, CHUNK), :]
            else:
                s_weight = roll(n_weight, 1, 0)
                if complete:
                    s_weight = jnp.where(
                        rows_of((CHUNK, LANES)) == 0, srows[pl.ds(nplane + 1, 1), :], s_weight
                    )
            ke, kw, kn, ks = k * e_weight, k * w_weight, k * n_weight, k * s_weight
            coef[0, piece, :] = 1.0 - ((ke + kw) + (kn + ks))
            coef[1, piece, :] = ke
            coef[2, piece, :] = kw
            coef[3, piece, :] = kn
            coef[4, piece, :] = ks

    set_coefficients(False)

    @pl.loop(0, nlevel)
    def _(level):
        def put(field, start, value):
            ext1[field * nlevel + level, pl.ds(PAD + start, CHUNK), :] = value

        advance(ext0, None, coef, nfield, nlevel, level, put)

    def arrived(dst, slot):
        remote(dst, dst, 0, slot, west, lat).wait_recv()

    arrived(recv_we.at[0], WEST)
    arrived(recv_we.at[1], EAST)
    arrived(recv_ns.at[1], NORTH)

    @pl.when(not_bottom)
    def _():
        arrived(recv_ns.at[0], SOUTH)
        arrived(recv_c.at[0], SOUTHWEST)
        arrived(recv_c.at[1], SOUTHEAST)

    @pl.when(ne_other)
    def _():
        arrived(recv_c.at[3], NORTHEAST)

    @pl.when(nw_other)
    def _():
        arrived(recv_c.at[2], NORTHWEST)

    go_w.wait_send()
    go_e.wait_send()
    go_n.wait_send()

    @pl.when(ne_other)
    def _():
        go_ne.wait_send()

    @pl.when(nw_other)
    def _():
        go_nw.wait_send()

    @pl.when(not_bottom)
    def _():
        go_s.wait_send()
        go_se.wait_send()
        go_sw.wait_send()

    def at_top(shape):
        return jnp.full(shape, lat, jnp.int32) == nlat - 1

    shape = (64, LANES)
    came = recv_ns[1, pl.ds(0, 64), :]
    sub = rows_of(shape) % 32
    flips = jnp.where(jnp.logical_and(sub >= 4 * nlevel, sub < nplane), -1.0, 1.0)
    nrows[...] = jnp.where(
        at_top(shape), flips * take_lanes(came, LANES - 1 - lanes_of(shape)), came
    )
    srows[...] = recv_ns[0, pl.ds(0, 64), :]

    eight = (8, LANES)
    lane8 = lanes_of(eight)
    slot8 = lane8 % 4
    flip8 = jnp.where(jnp.logical_and(lane8 >= 16 * nlevel, lane8 < 4 * nplane), -1.0, 1.0)
    east8 = lane8 // 4 == nplane

    def beyond(block):
        upside = jnp.concatenate([block[7 - i : 8 - i, :] for i in range(8)], axis=0)
        mirrored = flip8 * take_lanes(upside, lane8 - slot8 + (3 - slot8))
        mirrored = jnp.where(east8, roll(mirrored, -1, 1), mirrored)
        return mirrored

    middle_n = recv_ns[1, pl.ds(64, 8), :]
    middle_s = recv_ns[0, pl.ds(64, 8), :]
    slot = lane_h % 4
    place = 2 * (lane_h // 4) + lane_h % 2
    for start in (0, half):
        piece = pl.ds(start, half)
        own, at = packed[piece, :], place + (64 if start else 0)
        strips[0, pl.ds(PAD + start, half), :] = jnp.where(slot < 2, take_lanes(recv_we[0], at), own)
        strips[1, pl.ds(PAD + start, half), :] = jnp.where(slot < 2, own, take_lanes(recv_we[1], at))
    strips[0, pl.ds(0, 8), :] = jnp.where(slot8 < 2, recv_c[0], middle_s)
    strips[1, pl.ds(0, 8), :] = jnp.where(slot8 < 2, middle_s, recv_c[1])
    for side in range(2):
        lower, upper = ((recv_c[2], middle_n), (middle_n, recv_c[3]))[side]
        strips[side, pl.ds(top_row, 8), :] = jnp.where(
            at_top(eight),
            beyond(jnp.where(slot8 >= 2, lower, upper)),
            jnp.where(slot8 < 2, lower, upper),
        )

    tall = (rows + 2 * PAD, LANES)
    slot_t = lanes_of(tall) % 4
    lane_t = lanes_of(tall)
    folded = jnp.logical_and(at_top(tall), rows_of(tall) == top_row)

    def halo_of(west_strip, east_strip):
        return jnp.where(slot_t == 1, west_strip, roll(east_strip, -2, 1))

    advanced = []
    for side in range(2):
        x = strips[side]
        u = take_lanes(x, 16 * nlevel + lane_t % (4 * nlevel))
        v = take_lanes(x, 20 * nlevel + lane_t % (4 * nlevel))
        e_weight, n_weight, k = (
            take_lanes(x, 4 * (nplane + i) + slot_t) for i in range(3)
        )
        n_behind = roll(n_weight, 1, 0)
        n_south = jnp.where(folded, n_weight, n_behind)
        n_north = jnp.where(folded, roll(n_weight, -1, 0), n_weight)
        ke, kw, kn, ks = k * e_weight, k * roll(e_weight, 1, 1), k * n_north, k * n_south
        base = 1.0 - ((ke + kw) + (kn + ks))
        c = coefficients(
            base, ke, kw, kn, ks,
            u, roll(u, 1, 1), roll(u, -1, 1), v, roll(v, 1, 0), roll(v, -1, 0),
        )
        advanced.append(
            stencil(c, x, roll(x, 1, 1), roll(x, -1, 1), roll(x, 1, 0), roll(x, -1, 0))
        )
    halo1[...] = halo_of(advanced[0], advanced[1])
    edges[...] = roll(jnp.where(slot_t == 1, advanced[1], advanced[0]), -1, 1)
    set_coefficients(True)

    at_u, at_v = slice(4 * nlevel, 5 * nlevel), slice(5 * nlevel, 6 * nlevel)
    folded_1 = at_top((1, LANES))

    def spread(value):
        return jnp.concatenate([value] * nfield, axis=0)

    def set_row(row, x, south, north, k, e_weight, n_south, n_north):
        left, right = roll(x, 1, 1), roll(x, -1, 1)
        ke, kw = k * e_weight, k * roll(e_weight, 1, 1)
        kn, ks = k * n_north, k * n_south
        base = 1.0 - ((ke + kw) + (kn + ks))
        c = coefficients(
            base, ke, kw, kn, ks,
            spread(x[at_u]), spread(left[at_u]), spread(right[at_u]),
            spread(x[at_v]), spread(south[at_v]), spread(north[at_v]),
        )
        edge_rows[...] = stencil(c, x, left, right, south, north)
        for p in range(nplane):
            ext1[p, pl.ds(row, 1), :] = edge_rows[pl.ds(p, 1), :]

    def own_weights(buf):
        return buf[pl.ds(nplane + 2, 1), :], buf[pl.ds(nplane, 1), :], buf[pl.ds(nplane + 1, 1), :]

    inside, within = send_s[pl.ds(0, nplane), :], send_s[pl.ds(32, nplane), :]
    near, far = srows[pl.ds(0, nplane), :], srows[pl.ds(32, nplane), :]
    k, e_weight, n_weight = own_weights(send_s)
    k_near, e_near, n_near = own_weights(srows)
    n_far = srows[pl.ds(32 + nplane + 1, 1), :]
    set_row(PAD, inside, near, within, k, e_weight, n_near, n_weight)
    set_row(low_row, near, far, inside, k_near, e_near, n_far, n_near)

    inside, within = send_n[pl.ds(0, nplane), :], send_n[pl.ds(32, nplane), :]
    near, far = nrows[pl.ds(0, nplane), :], nrows[pl.ds(32, nplane), :]
    k, e_weight, n_weight = own_weights(send_n)
    n_within = send_n[pl.ds(32 + nplane + 1, 1), :]
    k_near, e_near, n_near = own_weights(nrows)
    e_near = jnp.where(folded_1, roll(e_near, -1, 1), e_near)
    n_far = nrows[pl.ds(32 + nplane + 1, 1), :]
    set_row(top_row - 1, inside, within, near, k, e_weight, n_within, n_weight)
    set_row(
        top_row, near, inside, far, k_near, e_near,
        jnp.where(folded_1, n_near, n_weight), jnp.where(folded_1, n_far, n_near),
    )

    lane_t = lanes_of(tall)
    is_edge = jnp.logical_or(lane_t == 0, lane_t == LANES - 1)
    at_edges = edges[...]
    for p in range(nplane):
        ext1[p] = jnp.where(is_edge, roll(at_edges, LANES - 1 - 4 * p, 1), ext1[p])


def second_kernel(nfield, nlevel, ext1, halo1, coef, out, obuf, out_sems):
    def store(level):
        return pltpu.make_async_copy(obuf.at[level], out.at[:, level], out_sems.at[level])

    @pl.loop(0, nlevel)
    def _(level):
        def put(field, start, value):
            obuf[level, field, pl.ds(start, CHUNK), :] = value

        advance(ext1, halo1, coef, nfield, nlevel, level, put)
        store(level).start()

    for level in range(nlevel):
        store(level).wait()


def solution(mesh):
    nlon, nlat = mesh.shape["lon"], mesh.shape["lat"]

    def local(fields, face_weights, inv_area, cell_mask, land_blocks):
        nfield, nlevel, rows, cols = fields.shape
        nplane = nfield * nlevel
        tall = rows + 2 * PAD
        f32 = jnp.float32
        anywhere = pl.BlockSpec(memory_space=pl.ANY)
        near = pl.BlockSpec(memory_space=pltpu.VMEM)

        def far(value):
            return pltpu.with_memory_space_constraint(value, pltpu.HBM)

        def first(*refs):
            first_kernel(nlon, nlat, nfield, nlevel, *refs)

        def second(*refs):
            second_kernel(nfield, nlevel, *refs)

        passed = pl.pallas_call(
            first,
            out_shape=[
                pltpu.VMEM((nplane, tall, cols), f32),
                pltpu.VMEM((tall, cols), f32),
                pltpu.VMEM((5, rows, cols), f32),
            ],
            in_specs=[anywhere] * 4 + [pl.BlockSpec(memory_space=pltpu.SMEM)],
            out_specs=[near] * 3,
            scratch_shapes=[
                pltpu.VMEM((nplane, tall, cols), f32),
                pltpu.VMEM((2, rows, cols), f32),
                pltpu.VMEM((rows, cols), f32),
                pltpu.VMEM((rows, cols), jnp.int32),
                pltpu.VMEM((rows, cols), f32),
                pltpu.VMEM((rows, cols), f32),
                pltpu.VMEM((72, cols), f32),
                pltpu.VMEM((72, cols), f32),
                pltpu.VMEM((2, rows // 2, cols), f32),
                pltpu.VMEM((2, rows // 2, cols), f32),
                pltpu.VMEM((2, 72, cols), f32),
                pltpu.VMEM((4, 8, cols), f32),
                pltpu.VMEM((tall, cols), f32),
                pltpu.VMEM((2, tall, cols), f32),
                pltpu.VMEM((64, cols), f32),
                pltpu.VMEM((64, cols), f32),
                pltpu.VMEM((nplane, cols), f32),
                pltpu.SemaphoreType.DMA((3 + rows // CHUNK,)),
                pltpu.SemaphoreType.DMA((8,)),
                pltpu.SemaphoreType.DMA((8,)),
            ],
            compiler_params=pltpu.CompilerParams(
                collective_id=0, has_side_effects=True, vmem_limit_bytes=16 * 1024 * 1024
            ),
        )(
            far(fields.reshape(nplane, rows, cols)), far(face_weights), far(inv_area),
            far(cell_mask), land_blocks,
        )
        return pl.pallas_call(
            second,
            out_shape=pltpu.HBM(fields.shape, f32),
            in_specs=[near] * 3,
            out_specs=anywhere,
            scratch_shapes=[
                pltpu.VMEM((nlevel, nfield, rows, cols), f32),
                pltpu.SemaphoreType.DMA((nlevel,)),
            ],
            compiler_params=pltpu.CompilerParams(vmem_limit_bytes=16 * 1024 * 1024),
        )(*(pltpu.with_memory_space_constraint(value, pltpu.VMEM) for value in passed))

    in_specs = (
        P(None, None, "lat", "lon"),
        P(None, "lat", "lon"),
        P("lat", "lon"),
        P("lat", "lon"),
        P("lat", "lon"),
    )
    out_specs = P(None, None, "lat", "lon")
    return jax.shard_map(local, mesh=mesh, in_specs=in_specs, out_specs=out_specs, check_vma=False)
```

```python
import jax
import jax.numpy as jnp
from jax import lax
from jax.experimental import pallas as pl
from jax.experimental.pallas import tpu as pltpu
from jax.sharding import PartitionSpec as P

TIME_STEP = 0.1
PAD = 8
CHUNK = 32
LANES = 128
WEST, EAST, SOUTH, NORTH, SOUTHWEST, SOUTHEAST, NORTHWEST, NORTHEAST = range(8)


def lanes_of(shape):
    return lax.broadcasted_iota(jnp.int32, shape, len(shape) - 1)


def rows_of(shape):
    return lax.broadcasted_iota(jnp.int32, shape, len(shape) - 2)


def roll(value, shift, axis):
    return pltpu.roll(value, shift % value.shape[axis], axis)


def take_lanes(value, index):
    return jnp.take_along_axis(value, index, axis=1)


def stencil(c, x, left, right, south, north):
    c0, ce, cw, cn, cs = c
    return c0 * x + ce * right + cw * left + cn * north + cs * south


def coefficients(base, ke, kw, kn, ks, u, u_left, u_right, v, v_south, v_north):
    pe = ke * (0.125 * (u + u_right))
    pw = kw * (0.125 * (u + u_left))
    pn = kn * (0.125 * (v + v_north))
    ps = ks * (0.125 * (v + v_south))
    return base + ((pw - pe) + (ps - pn)), ke - pe, kw + pw, kn - pn, ks + ps


def advance(source, coef, nfield, nlevel, level, put):
    rows = coef.shape[1]
    for start in range(0, rows, CHUNK):
        piece = pl.ds(start, CHUNK)
        base, ke, kw, kn, ks = (coef[i, piece, :] for i in range(5))

        def centre(field):
            return source[field * nlevel + level, pl.ds(PAD + start, CHUNK), :]

        def columns_beside(x):
            return roll(x, 1, 1), roll(x, -1, 1)

        def rows_beside(field):
            return (
                source[field * nlevel + level, pl.ds(PAD + start - 1, CHUNK), :],
                source[field * nlevel + level, pl.ds(PAD + start + 1, CHUNK), :],
            )

        u, v = centre(4), centre(5)
        u_sides, v_sides = columns_beside(u), rows_beside(5)
        c = coefficients(base, ke, kw, kn, ks, u, *u_sides, v, *v_sides)
        for field in range(nfield):
            x = centre(field)
            left, right = u_sides if field == 4 else columns_beside(x)
            south, north = v_sides if field == 5 else rows_beside(field)
            put(field, start, stencil(c, x, left, right, south, north))


def first_kernel(
    nlon, nlat, nfield, nlevel,
    fields, face_weights, inv_area, cell_mask, land,
    state, columns,
    ext0, ext1, coef, weights, area, cells, scale, packed, send_s, send_n,
    send_we, recv_we, recv_ns, recv_c, inner, strips, nrows, srows, edge_rows,
    in_sems, send_sems, recv_sems,
):
    nplane = nfield * nlevel
    rows = ext0.shape[1] - 2 * PAD
    top_row, low_row = PAD + rows, PAD - 1
    lon, lat = lax.axis_index("lon"), lax.axis_index("lat")
    is_top = lat == nlat - 1
    is_bottom = lat == 0
    east, west = lax.rem(lon + 1, nlon), lax.rem(lon + nlon - 1, nlon)
    north_lat = jnp.where(is_top, lat, lat + 1)
    north_lon = jnp.where(is_top, nlon - 1 - lon, lon)
    ne_lon = jnp.where(is_top, lax.rem(2 * nlon - 2 - lon, nlon), east)
    nw_lon = jnp.where(is_top, lax.rem(nlon - lon, nlon), west)
    ne_self = jnp.logical_and(is_top, ne_lon == lon)
    nw_self = jnp.logical_and(is_top, nw_lon == lon)
    ne_other = jnp.logical_not(ne_self)
    nw_other = jnp.logical_not(nw_self)
    not_bottom = jnp.logical_not(is_bottom)

    barrier = pltpu.get_barrier_semaphore()

    def greet(to_lon, to_lat):
        pl.semaphore_signal(
            barrier, inc=1, device_id={"lon": to_lon, "lat": to_lat},
            device_id_type=pl.DeviceIdType.MESH,
        )

    greet(west, lat)
    greet(east, lat)
    greet(north_lon, north_lat)

    @pl.when(ne_other)
    def _():
        greet(ne_lon, north_lat)

    @pl.when(nw_other)
    def _():
        greet(nw_lon, north_lat)

    @pl.when(not_bottom)
    def _():
        greet(lon, lat - 1)
        greet(east, lat - 1)
        greet(west, lat - 1)

    starts = range(0, rows, CHUNK)
    loads = [
        pltpu.make_async_copy(face_weights, weights, in_sems.at[0]),
        pltpu.make_async_copy(inv_area, area, in_sems.at[1]),
        pltpu.make_async_copy(cell_mask, cells, in_sems.at[2]),
    ]
    pieces = [
        pltpu.make_async_copy(
            fields.at[:, pl.ds(start, CHUNK), :], ext0.at[:, pl.ds(PAD + start, CHUNK), :],
            in_sems.at[3 + i],
        )
        for i, start in enumerate(starts)
    ]
    for load in loads + pieces:
        load.start()
    for load in loads:
        load.wait()
    sea = (1 - land[0, 0]).astype(jnp.float32)
    scale[...] = (TIME_STEP * sea) * cells[...].astype(jnp.float32) * area[...]

    group = lanes_of((CHUNK, LANES)) // 4
    for start, load in zip(starts, pieces):
        piece = pl.ds(start, CHUNK)
        load.wait()
        gathered = jnp.zeros((CHUNK, LANES), jnp.float32)
        for p in range(nplane + 3):
            if p < nplane:
                plane = ext0[p, pl.ds(PAD + start, CHUNK), :]
            elif p < nplane + 2:
                plane = weights[p - nplane, piece, :]
            else:
                plane = scale[piece, :]
            gathered = jnp.where(group == p, roll(plane, 4 * p + 2, 1), gathered)
        packed[piece, :] = gathered
    half = rows // 2
    lane_h = lanes_of((half, LANES))
    pick = 4 * ((lane_h % 64) // 2) + lane_h % 2
    for side in range(2):
        send_we[side] = jnp.where(
            lane_h < 64,
            take_lanes(packed[pl.ds(0, half), :], pick + 2 * side),
            take_lanes(packed[pl.ds(half, half), :], pick + 2 * side),
        )
    for buf, first, second, corner in ((send_s, 0, 1, 0), (send_n, rows - 1, rows - 2, rows - 8)):
        for at, row in ((0, first), (32, second)):
            for p in range(nplane):
                buf[pl.ds(at + p, 1), :] = ext0[p, pl.ds(PAD + row, 1), :]
            for i in range(2):
                buf[pl.ds(at + nplane + i, 1), :] = weights[i, pl.ds(row, 1), :]
            buf[pl.ds(at + nplane + 2, 1), :] = scale[pl.ds(row, 1), :]
            buf[pl.ds(at + nplane + 3, 5), :] = jnp.zeros((5, LANES), jnp.float32)
        buf[pl.ds(64, 8), :] = packed[pl.ds(corner, 8), :]

    def remote(src, dst, number, slot, to_lon, to_lat):
        return pltpu.make_async_remote_copy(
            src_ref=src, dst_ref=dst, send_sem=send_sems.at[number], recv_sem=recv_sems.at[slot],
            device_id={"lon": to_lon, "lat": to_lat}, device_id_type=pl.DeviceIdType.MESH,
        )

    corner_s, corner_n = send_s.at[pl.ds(64, 8), :], send_n.at[pl.ds(64, 8), :]
    go_w = remote(send_we.at[1], recv_we.at[1], 0, EAST, west, lat)
    go_e = remote(send_we.at[0], recv_we.at[0], 1, WEST, east, lat)
    go_n = remote(
        send_n, recv_ns.at[jnp.where(is_top, 1, 0)], 2,
        jnp.where(is_top, NORTH, SOUTH), north_lon, north_lat,
    )
    go_ne = remote(
        corner_n, recv_c.at[jnp.where(is_top, 3, 0)], 3,
        jnp.where(is_top, NORTHEAST, SOUTHWEST), ne_lon, north_lat,
    )
    go_nw = remote(
        corner_n, recv_c.at[jnp.where(is_top, 2, 1)], 4,
        jnp.where(is_top, NORTHWEST, SOUTHEAST), nw_lon, north_lat,
    )
    go_s = remote(send_s, recv_ns.at[1], 5, NORTH, lon, lat - 1)
    go_se = remote(corner_s, recv_c.at[2], 6, NORTHWEST, east, lat - 1)
    go_sw = remote(corner_s, recv_c.at[3], 7, NORTHEAST, west, lat - 1)

    greetings = 3 + jnp.where(ne_self, 0, 1) + jnp.where(nw_self, 0, 1) + jnp.where(is_bottom, 0, 3)
    pl.semaphore_wait(barrier, greetings)
    go_w.start()
    go_e.start()
    go_n.start()

    @pl.when(ne_other)
    def _():
        go_ne.start()

    @pl.when(nw_other)
    def _():
        go_nw.start()

    @pl.when(not_bottom)
    def _():
        go_s.start()
        go_se.start()
        go_sw.start()

    @pl.when(ne_self)
    def _():
        recv_c[3] = send_n[pl.ds(64, 8), :]

    @pl.when(nw_self)
    def _():
        recv_c[2] = send_n[pl.ds(64, 8), :]

    @pl.when(is_bottom)
    def _():
        recv_ns[0] = jnp.zeros(recv_ns.shape[1:], jnp.float32)
        recv_c[0] = jnp.zeros(recv_c.shape[1:], jnp.float32)
        recv_c[1] = jnp.zeros(recv_c.shape[1:], jnp.float32)

    def set_coefficients(start, row_before):
        piece = pl.ds(start, CHUNK)
        k = scale[piece, :]
        e_weight = weights[0, piece, :]
        n_weight = weights[1, piece, :]
        w_weight = roll(e_weight, 1, 1)
        if start:
            s_weight = weights[1, pl.ds(start - 1, CHUNK), :]
        else:
            s_weight = roll(n_weight, 1, 0)
            if row_before is not None:
                s_weight = jnp.where(rows_of((CHUNK, LANES)) == 0, row_before, s_weight)
        ke, kw, kn, ks = k * e_weight, k * w_weight, k * n_weight, k * s_weight
        coef[0, piece, :] = 1.0 - ((ke + kw) + (kn + ks))
        coef[1, piece, :] = ke
        coef[2, piece, :] = kw
        coef[3, piece, :] = kn
        coef[4, piece, :] = ks

    for start in starts:
        set_coefficients(start, None)

    @pl.loop(0, nlevel)
    def _(level):
        def put(field, start, value):
            ext1[field * nlevel + level, pl.ds(PAD + start, CHUNK), :] = value

        advance(ext0, coef, nfield, nlevel, level, put)

    def arrived(dst, slot):
        remote(dst, dst, 0, slot, west, lat).wait_recv()

    arrived(recv_ns.at[1], NORTH)

    @pl.when(not_bottom)
    def _():
        arrived(recv_ns.at[0], SOUTH)

    def at_top(shape):
        return jnp.full(shape, lat, jnp.int32) == nlat - 1

    shape = (64, LANES)
    came = recv_ns[1, pl.ds(0, 64), :]
    sub = rows_of(shape) % 32
    flips = jnp.where(jnp.logical_and(sub >= 4 * nlevel, sub < nplane), -1.0, 1.0)
    nrows[...] = jnp.where(
        at_top(shape), flips * take_lanes(came, LANES - 1 - lanes_of(shape)), came
    )
    srows[...] = recv_ns[0, pl.ds(0, 64), :]

    at_u, at_v = slice(4 * nlevel, 5 * nlevel), slice(5 * nlevel, 6 * nlevel)
    folded_1 = at_top((1, LANES))

    def spread(value):
        return jnp.concatenate([value] * nfield, axis=0)

    def set_row(row, x, south, north, k, e_weight, n_south, n_north):
        left, right = roll(x, 1, 1), roll(x, -1, 1)
        ke, kw = k * e_weight, k * roll(e_weight, 1, 1)
        kn, ks = k * n_north, k * n_south
        base = 1.0 - ((ke + kw) + (kn + ks))
        c = coefficients(
            base, ke, kw, kn, ks,
            spread(x[at_u]), spread(left[at_u]), spread(right[at_u]),
            spread(x[at_v]), spread(south[at_v]), spread(north[at_v]),
        )
        edge_rows[...] = stencil(c, x, left, right, south, north)
        for p in range(nplane):
            ext1[p, pl.ds(row, 1), :] = edge_rows[pl.ds(p, 1), :]

    def own_weights(buf):
        return buf[pl.ds(nplane + 2, 1), :], buf[pl.ds(nplane, 1), :], buf[pl.ds(nplane + 1, 1), :]

    inside, within = send_s[pl.ds(0, nplane), :], send_s[pl.ds(32, nplane), :]
    near, far = srows[pl.ds(0, nplane), :], srows[pl.ds(32, nplane), :]
    k, e_weight, n_weight = own_weights(send_s)
    k_near, e_near, n_near = own_weights(srows)
    n_far = srows[pl.ds(32 + nplane + 1, 1), :]
    set_row(PAD, inside, near, within, k, e_weight, n_near, n_weight)
    set_row(low_row, near, far, inside, k_near, e_near, n_far, n_near)

    inside, within = send_n[pl.ds(0, nplane), :], send_n[pl.ds(32, nplane), :]
    near, far = nrows[pl.ds(0, nplane), :], nrows[pl.ds(32, nplane), :]
    k, e_weight, n_weight = own_weights(send_n)
    n_within = send_n[pl.ds(32 + nplane + 1, 1), :]
    k_near, e_near, n_near = own_weights(nrows)
    e_near = jnp.where(folded_1, roll(e_near, -1, 1), e_near)
    n_far = nrows[pl.ds(32 + nplane + 1, 1), :]
    set_row(top_row - 1, inside, within, near, k, e_weight, n_within, n_weight)
    set_row(
        top_row, near, inside, far, k_near, e_near,
        jnp.where(folded_1, n_near, n_weight), jnp.where(folded_1, n_far, n_near),
    )

    set_coefficients(0, srows[pl.ds(nplane + 1, 1), :])

    @pl.loop(0, nlevel)
    def _(level):
        def put(field, start, value):
            state[field * nlevel + level, pl.ds(start, CHUNK), :] = value

        advance(ext1, coef, nfield, nlevel, level, put)

    for start in range(0, rows + 2 * PAD, 48):
        piece = pl.ds(start, 48)
        lane = lanes_of((48, LANES))
        gathered = jnp.zeros((48, LANES), jnp.float32)
        for p in range(nplane):
            plane = ext1[p, piece, :]
            gathered = jnp.where(lane // 2 == 2 * p, roll(plane, 4 * p + 3, 1), gathered)
            gathered = jnp.where(lane // 2 == 2 * p + 1, roll(plane, 4 * p + 1, 1), gathered)
        inner[piece, :] = gathered

    arrived(recv_we.at[0], WEST)
    arrived(recv_we.at[1], EAST)

    @pl.when(not_bottom)
    def _():
        arrived(recv_c.at[0], SOUTHWEST)
        arrived(recv_c.at[1], SOUTHEAST)

    @pl.when(ne_other)
    def _():
        arrived(recv_c.at[3], NORTHEAST)

    @pl.when(nw_other)
    def _():
        arrived(recv_c.at[2], NORTHWEST)

    eight = (8, LANES)
    lane8 = lanes_of(eight)
    slot8 = lane8 % 4
    flip8 = jnp.where(jnp.logical_and(lane8 >= 16 * nlevel, lane8 < 4 * nplane), -1.0, 1.0)
    east8 = lane8 // 4 == nplane

    def beyond(block):
        upside = jnp.concatenate([block[7 - i : 8 - i, :] for i in range(8)], axis=0)
        mirrored = flip8 * take_lanes(upside, lane8 - slot8 + (3 - slot8))
        mirrored = jnp.where(east8, roll(mirrored, -1, 1), mirrored)
        return mirrored

    middle_n = recv_ns[1, pl.ds(64, 8), :]
    middle_s = recv_ns[0, pl.ds(64, 8), :]
    slot = lane_h % 4
    place = 2 * (lane_h // 4) + lane_h % 2
    for start in (0, half):
        piece = pl.ds(start, half)
        own, at = packed[piece, :], place + (64 if start else 0)
        strips[0, pl.ds(PAD + start, half), :] = jnp.where(slot < 2, take_lanes(recv_we[0], at), own)
        strips[1, pl.ds(PAD + start, half), :] = jnp.where(slot < 2, own, take_lanes(recv_we[1], at))
    strips[0, pl.ds(0, 8), :] = jnp.where(slot8 < 2, recv_c[0], middle_s)
    strips[1, pl.ds(0, 8), :] = jnp.where(slot8 < 2, middle_s, recv_c[1])
    for side in range(2):
        lower, upper = ((recv_c[2], middle_n), (middle_n, recv_c[3]))[side]
        strips[side, pl.ds(top_row, 8), :] = jnp.where(
            at_top(eight),
            beyond(jnp.where(slot8 >= 2, lower, upper)),
            jnp.where(slot8 < 2, lower, upper),
        )

    tall = (rows + 2 * PAD, LANES)
    slot_t = lanes_of(tall) % 4
    lane_t = lanes_of(tall)
    folded = jnp.logical_and(at_top(tall), rows_of(tall) == top_row)

    beyond_125 = take_lanes(weights[0], jnp.full((rows, LANES), LANES - 3, jnp.int32))
    beyond_125 = jnp.concatenate([beyond_125[:PAD], beyond_125, beyond_125[:PAD]], axis=0)
    inner_all = inner[...]
    index_u = 16 * nlevel + lane_t % (4 * nlevel)
    index_v = 20 * nlevel + lane_t % (4 * nlevel)

    def strip_step(w, x, left, right):
        south, north = roll(x, 1, 0), roll(x, -1, 0)
        u = take_lanes(x, index_u), take_lanes(left, index_u), take_lanes(right, index_u)
        v = take_lanes(x, index_v)
        c = coefficients(*w, *u, v, roll(v, 1, 0), roll(v, -1, 0))
        return stencil(c, x, left, right, south, north)

    advanced = []
    for side in range(2):
        x = strips[side]
        e_weight, n_weight, k = (
            take_lanes(x, 4 * (nplane + i) + slot_t) for i in range(3)
        )
        w_weight = jnp.where(slot_t == 0, beyond_125, roll(e_weight, 1, 1))
        n_south = jnp.where(folded, n_weight, roll(n_weight, 1, 0))
        n_north = jnp.where(folded, roll(n_weight, -1, 0), n_weight)
        ke, kw, kn, ks = k * e_weight, k * w_weight, k * n_north, k * n_south
        w = (1.0 - ((ke + kw) + (kn + ks)), ke, kw, kn, ks)
        x = strip_step(w, x, roll(x, 1, 1), roll(x, -1, 1))
        x = jnp.where(
            slot_t == 0, roll(inner_all, -1, 1), jnp.where(slot_t == 3, roll(inner_all, 1, 1), x)
        )
        left = jnp.where(slot_t == 0, inner_all, roll(x, 1, 1))
        right = jnp.where(slot_t == 3, inner_all, roll(x, -1, 1))
        advanced.append(strip_step(w, x, left, right))
    final = jnp.where(slot_t < 2, advanced[1], advanced[0])
    columns[...] = final[PAD : PAD + rows, :]

    go_w.wait_send()
    go_e.wait_send()
    go_n.wait_send()

    @pl.when(ne_other)
    def _():
        go_ne.wait_send()

    @pl.when(nw_other)
    def _():
        go_nw.wait_send()

    @pl.when(not_bottom)
    def _():
        go_s.wait_send()
        go_se.wait_send()
        go_sw.wait_send()


def second_kernel(state, columns, out, obuf, out_sems):
    nplane, rows, cols = state.shape
    lane = lanes_of((rows, cols))
    is_edge = jnp.logical_or(lane < 2, lane >= LANES - 2)
    parts = out_sems.shape[0]
    size = nplane // parts
    copies = []
    for part in range(parts):
        for p in range(part * size, (part + 1) * size):
            obuf[p] = jnp.where(is_edge, roll(columns[...], -(4 * p + 2), 1), state[p])
        piece = pl.ds(part * size, size)
        copies.append(pltpu.make_async_copy(obuf.at[piece], out.at[piece], out_sems.at[part]))
        copies[-1].start()
    for copy in copies:
        copy.wait()


def solution(mesh):
    nlon, nlat = mesh.shape["lon"], mesh.shape["lat"]

    def local(fields, face_weights, inv_area, cell_mask, land_blocks):
        nfield, nlevel, rows, cols = fields.shape
        nplane = nfield * nlevel
        tall = rows + 2 * PAD
        f32 = jnp.float32
        anywhere = pl.BlockSpec(memory_space=pl.ANY)
        near = pl.BlockSpec(memory_space=pltpu.VMEM)

        def far(value):
            return pltpu.with_memory_space_constraint(value, pltpu.HBM)

        def first(*refs):
            first_kernel(nlon, nlat, nfield, nlevel, *refs)

        def second(*refs):
            second_kernel(*refs)

        passed = pl.pallas_call(
            first,
            out_shape=[
                pltpu.VMEM((nplane, rows, cols), f32),
                pltpu.VMEM((rows, cols), f32),
            ],
            in_specs=[anywhere] * 4 + [pl.BlockSpec(memory_space=pltpu.SMEM)],
            out_specs=[near] * 2,
            scratch_shapes=[
                pltpu.VMEM((nplane, tall, cols), f32),
                pltpu.VMEM((nplane, tall, cols), f32),
                pltpu.VMEM((5, rows, cols), f32),
                pltpu.VMEM((2, rows, cols), f32),
                pltpu.VMEM((rows, cols), f32),
                pltpu.VMEM((rows, cols), jnp.int32),
                pltpu.VMEM((rows, cols), f32),
                pltpu.VMEM((rows, cols), f32),
                pltpu.VMEM((72, cols), f32),
                pltpu.VMEM((72, cols), f32),
                pltpu.VMEM((2, rows // 2, cols), f32),
                pltpu.VMEM((2, rows // 2, cols), f32),
                pltpu.VMEM((2, 72, cols), f32),
                pltpu.VMEM((4, 8, cols), f32),
                pltpu.VMEM((tall, cols), f32),
                pltpu.VMEM((2, tall, cols), f32),
                pltpu.VMEM((64, cols), f32),
                pltpu.VMEM((64, cols), f32),
                pltpu.VMEM((nplane, cols), f32),
                pltpu.SemaphoreType.DMA((3 + rows // CHUNK,)),
                pltpu.SemaphoreType.DMA((8,)),
                pltpu.SemaphoreType.DMA((8,)),
            ],
            compiler_params=pltpu.CompilerParams(
                collective_id=0, has_side_effects=True, vmem_limit_bytes=16 * 1024 * 1024
            ),
        )(
            far(fields.reshape(nplane, rows, cols)), far(face_weights), far(inv_area),
            far(cell_mask), land_blocks,
        )
        result = pl.pallas_call(
            second,
            out_shape=pltpu.HBM((nplane, rows, cols), f32),
            in_specs=[near] * 2,
            out_specs=anywhere,
            scratch_shapes=[
                pltpu.VMEM((nplane, rows, cols), f32),
                pltpu.SemaphoreType.DMA((4,)),
            ],
            compiler_params=pltpu.CompilerParams(vmem_limit_bytes=16 * 1024 * 1024),
        )(*(pltpu.with_memory_space_constraint(value, pltpu.VMEM) for value in passed))
        return result.reshape(fields.shape)

    in_specs = (
        P(None, None, "lat", "lon"),
        P(None, "lat", "lon"),
        P("lat", "lon"),
        P("lat", "lon"),
        P("lat", "lon"),
    )
    out_specs = P(None, None, "lat", "lon")
    return jax.shard_map(local, mesh=mesh, in_specs=in_specs, out_specs=out_specs, check_vma=False)
```

```python
import jax
import jax.numpy as jnp
from jax import lax
from jax.experimental import pallas as pl
from jax.experimental.pallas import tpu as pltpu
from jax.sharding import PartitionSpec as P

TIME_STEP = 0.1
PAD = 8
CHUNK = 32
LANES = 128
WEST, EAST, SOUTH, NORTH, SOUTHWEST, SOUTHEAST, NORTHWEST, NORTHEAST = range(8)


def lanes_of(shape):
    return lax.broadcasted_iota(jnp.int32, shape, len(shape) - 1)


def rows_of(shape):
    return lax.broadcasted_iota(jnp.int32, shape, len(shape) - 2)


def roll(value, shift, axis):
    return pltpu.roll(value, shift % value.shape[axis], axis)


def take_lanes(value, index):
    return jnp.take_along_axis(value, index, axis=1)


def stencil(c, x, left, right, south, north):
    c0, ce, cw, cn, cs = c
    return c0 * x + ce * right + cw * left + cn * north + cs * south


def coefficients(base, ke, kw, kn, ks, u, u_left, u_right, v, v_south, v_north):
    pe = ke * (0.125 * (u + u_right))
    pw = kw * (0.125 * (u + u_left))
    pn = kn * (0.125 * (v + v_north))
    ps = ks * (0.125 * (v + v_south))
    return base + ((pw - pe) + (ps - pn)), ke - pe, kw + pw, kn - pn, ks + ps


def advance(source, coef, nfield, nlevel, level, put):
    rows = coef.shape[1]
    for start in range(0, rows, CHUNK):
        piece = pl.ds(start, CHUNK)
        base, ke, kw, kn, ks = (coef[i, piece, :] for i in range(5))

        def centre(field):
            return source[field * nlevel + level, pl.ds(PAD + start, CHUNK), :]

        def columns_beside(x):
            return roll(x, 1, 1), roll(x, -1, 1)

        def rows_beside(field):
            return (
                source[field * nlevel + level, pl.ds(PAD + start - 1, CHUNK), :],
                source[field * nlevel + level, pl.ds(PAD + start + 1, CHUNK), :],
            )

        u, v = centre(4), centre(5)
        u_sides, v_sides = columns_beside(u), rows_beside(5)
        c = coefficients(base, ke, kw, kn, ks, u, *u_sides, v, *v_sides)
        for field in range(nfield):
            x = centre(field)
            left, right = u_sides if field == 4 else columns_beside(x)
            south, north = v_sides if field == 5 else rows_beside(field)
            put(field, start, stencil(c, x, left, right, south, north))


def first_kernel(
    nlon, nlat, nfield, nlevel,
    fields, face_weights, inv_area, cell_mask, land,
    state, columns,
    ext0, ext1, coef, weights, area, cells, scale, packed, send_s, send_n,
    send_we, recv_we, recv_ns, recv_c, inner, strips, nrows, srows, edge_rows,
    in_sems, send_sems, recv_sems,
):
    nplane = nfield * nlevel
    rows = ext0.shape[1] - 2 * PAD
    top_row, low_row = PAD + rows, PAD - 1
    lon, lat = lax.axis_index("lon"), lax.axis_index("lat")
    is_top = lat == nlat - 1
    is_bottom = lat == 0
    east, west = lax.rem(lon + 1, nlon), lax.rem(lon + nlon - 1, nlon)
    north_lat = jnp.where(is_top, lat, lat + 1)
    north_lon = jnp.where(is_top, nlon - 1 - lon, lon)
    ne_lon = jnp.where(is_top, lax.rem(2 * nlon - 2 - lon, nlon), east)
    nw_lon = jnp.where(is_top, lax.rem(nlon - lon, nlon), west)
    ne_self = jnp.logical_and(is_top, ne_lon == lon)
    nw_self = jnp.logical_and(is_top, nw_lon == lon)
    ne_other = jnp.logical_not(ne_self)
    nw_other = jnp.logical_not(nw_self)
    not_bottom = jnp.logical_not(is_bottom)

    barrier = pltpu.get_barrier_semaphore()

    def greet(to_lon, to_lat):
        pl.semaphore_signal(
            barrier, inc=1, device_id={"lon": to_lon, "lat": to_lat},
            device_id_type=pl.DeviceIdType.MESH,
        )

    greet(west, lat)
    greet(east, lat)
    greet(north_lon, north_lat)

    @pl.when(ne_other)
    def _():
        greet(ne_lon, north_lat)

    @pl.when(nw_other)
    def _():
        greet(nw_lon, north_lat)

    @pl.when(not_bottom)
    def _():
        greet(lon, lat - 1)
        greet(east, lat - 1)
        greet(west, lat - 1)

    starts = range(0, rows, CHUNK)
    loads = [
        pltpu.make_async_copy(face_weights, weights, in_sems.at[0]),
        pltpu.make_async_copy(inv_area, area, in_sems.at[1]),
        pltpu.make_async_copy(cell_mask, cells, in_sems.at[2]),
    ]
    pieces = [
        pltpu.make_async_copy(
            fields.at[:, pl.ds(start, CHUNK), :], ext0.at[:, pl.ds(PAD + start, CHUNK), :],
            in_sems.at[3 + i],
        )
        for i, start in enumerate(starts)
    ]
    for load in loads + pieces:
        load.start()
    for load in loads:
        load.wait()
    sea = (1 - land[0, 0]).astype(jnp.float32)
    scale[...] = (TIME_STEP * sea) * cells[...].astype(jnp.float32) * area[...]

    group = lanes_of((CHUNK, LANES)) // 4
    for start, load in zip(starts, pieces):
        piece = pl.ds(start, CHUNK)
        load.wait()
        gathered = jnp.zeros((CHUNK, LANES), jnp.float32)
        for p in range(nplane + 3):
            if p < nplane:
                plane = ext0[p, pl.ds(PAD + start, CHUNK), :]
            elif p < nplane + 2:
                plane = weights[p - nplane, piece, :]
            else:
                plane = scale[piece, :]
            gathered = jnp.where(group == p, roll(plane, 4 * p + 2, 1), gathered)
        packed[piece, :] = gathered
    half = rows // 2
    lane_h = lanes_of((half, LANES))
    pick = 4 * ((lane_h % 64) // 2) + lane_h % 2
    for side in range(2):
        send_we[side] = jnp.where(
            lane_h < 64,
            take_lanes(packed[pl.ds(0, half), :], pick + 2 * side),
            take_lanes(packed[pl.ds(half, half), :], pick + 2 * side),
        )
    for buf, first, second, corner in ((send_s, 0, 1, 0), (send_n, rows - 1, rows - 2, rows - 8)):
        for at, row in ((0, first), (28, second)):
            for p in range(nplane):
                buf[pl.ds(at + p, 1), :] = ext0[p, pl.ds(PAD + row, 1), :]
            for i in range(2):
                buf[pl.ds(at + nplane + i, 1), :] = weights[i, pl.ds(row, 1), :]
            buf[pl.ds(at + nplane + 2, 1), :] = scale[pl.ds(row, 1), :]
            buf[pl.ds(at + nplane + 3, 1), :] = jnp.zeros((1, LANES), jnp.float32)
        buf[pl.ds(56, 8), :] = packed[pl.ds(corner, 8), :]

    def remote(src, dst, number, slot, to_lon, to_lat):
        return pltpu.make_async_remote_copy(
            src_ref=src, dst_ref=dst, send_sem=send_sems.at[number], recv_sem=recv_sems.at[slot],
            device_id={"lon": to_lon, "lat": to_lat}, device_id_type=pl.DeviceIdType.MESH,
        )

    corner_s, corner_n = send_s.at[pl.ds(56, 8), :], send_n.at[pl.ds(56, 8), :]
    go_w = remote(send_we.at[1], recv_we.at[1], 0, EAST, west, lat)
    go_e = remote(send_we.at[0], recv_we.at[0], 1, WEST, east, lat)
    go_n = remote(
        send_n, recv_ns.at[jnp.where(is_top, 1, 0)], 2,
        jnp.where(is_top, NORTH, SOUTH), north_lon, north_lat,
    )
    go_ne = remote(
        corner_n, recv_c.at[jnp.where(is_top, 3, 0)], 3,
        jnp.where(is_top, NORTHEAST, SOUTHWEST), ne_lon, north_lat,
    )
    go_nw = remote(
        corner_n, recv_c.at[jnp.where(is_top, 2, 1)], 4,
        jnp.where(is_top, NORTHWEST, SOUTHEAST), nw_lon, north_lat,
    )
    go_s = remote(send_s, recv_ns.at[1], 5, NORTH, lon, lat - 1)
    go_se = remote(corner_s, recv_c.at[2], 6, NORTHWEST, east, lat - 1)
    go_sw = remote(corner_s, recv_c.at[3], 7, NORTHEAST, west, lat - 1)

    greetings = 3 + jnp.where(ne_self, 0, 1) + jnp.where(nw_self, 0, 1) + jnp.where(is_bottom, 0, 3)
    pl.semaphore_wait(barrier, greetings)
    go_n.start()
    go_w.start()
    go_e.start()

    @pl.when(ne_other)
    def _():
        go_ne.start()

    @pl.when(nw_other)
    def _():
        go_nw.start()

    @pl.when(not_bottom)
    def _():
        go_s.start()
        go_se.start()
        go_sw.start()

    @pl.when(ne_self)
    def _():
        recv_c[3] = send_n[pl.ds(56, 8), :]

    @pl.when(nw_self)
    def _():
        recv_c[2] = send_n[pl.ds(56, 8), :]

    @pl.when(is_bottom)
    def _():
        recv_ns[0] = jnp.zeros(recv_ns.shape[1:], jnp.float32)
        recv_c[0] = jnp.zeros(recv_c.shape[1:], jnp.float32)
        recv_c[1] = jnp.zeros(recv_c.shape[1:], jnp.float32)

    def set_coefficients(start):
        piece = pl.ds(start, CHUNK)
        k = scale[piece, :]
        e_weight = weights[0, piece, :]
        n_weight = weights[1, piece, :]
        w_weight = roll(e_weight, 1, 1)
        if start:
            s_weight = weights[1, pl.ds(start - 1, CHUNK), :]
        else:
            s_weight = roll(n_weight, 1, 0)
        ke, kw, kn, ks = k * e_weight, k * w_weight, k * n_weight, k * s_weight
        coef[0, piece, :] = 1.0 - ((ke + kw) + (kn + ks))
        coef[1, piece, :] = ke
        coef[2, piece, :] = kw
        coef[3, piece, :] = kn
        coef[4, piece, :] = ks

    for start in starts:
        set_coefficients(start)

    @pl.loop(0, nlevel)
    def _(level):
        def put(field, start, value):
            ext1[field * nlevel + level, pl.ds(PAD + start, CHUNK), :] = value

        advance(ext0, coef, nfield, nlevel, level, put)

    @pl.loop(0, nlevel)
    def _(level):
        def put(field, start, value):
            state[field * nlevel + level, pl.ds(start, CHUNK), :] = value

        advance(ext1, coef, nfield, nlevel, level, put)

    for start in range(0, rows + 2 * PAD, 48):
        piece = pl.ds(start, 48)
        lane = lanes_of((48, LANES))
        gathered = jnp.zeros((48, LANES), jnp.float32)
        for p in range(nplane):
            plane = ext1[p, piece, :]
            gathered = jnp.where(lane // 2 == 2 * p, roll(plane, 4 * p + 3, 1), gathered)
            gathered = jnp.where(lane // 2 == 2 * p + 1, roll(plane, 4 * p + 1, 1), gathered)
        inner[piece, :] = gathered

    for i, row in enumerate((PAD + 1, PAD + 2, top_row - 2, top_row - 3)):
        for p in range(nplane):
            edge_rows[i, pl.ds(p, 1), :] = ext1[p, pl.ds(row, 1), :]

    def arrived(dst, slot):
        remote(dst, dst, 0, slot, west, lat).wait_recv()

    arrived(recv_ns.at[1], NORTH)

    @pl.when(not_bottom)
    def _():
        arrived(recv_ns.at[0], SOUTH)

    def at_top(shape):
        return jnp.full(shape, lat, jnp.int32) == nlat - 1

    shape = (56, LANES)
    came = recv_ns[1, pl.ds(0, 56), :]
    sub = rows_of(shape) % 28
    flips = jnp.where(jnp.logical_and(sub >= 4 * nlevel, sub < nplane), -1.0, 1.0)
    nrows[...] = jnp.where(
        at_top(shape), flips * take_lanes(came, LANES - 1 - lanes_of(shape)), came
    )
    srows[...] = recv_ns[0, pl.ds(0, 56), :]

    at_u, at_v = slice(4 * nlevel, 5 * nlevel), slice(5 * nlevel, 6 * nlevel)
    folded_1 = at_top((1, LANES))
    flat = (nplane, LANES)
    lane_f = lanes_of(flat)
    slot_f = lane_f % 4
    column_f = jnp.where(slot_f < 2, LANES - 3 + slot_f, slot_f - 1)

    def spread(value):
        return jnp.concatenate([value] * nfield, axis=0)

    def row_step(x, south, north, k, e_weight, n_south, n_north):
        left, right = roll(x, 1, 1), roll(x, -1, 1)
        ke, kw = k * e_weight, k * roll(e_weight, 1, 1)
        kn, ks = k * n_north, k * n_south
        base = 1.0 - ((ke + kw) + (kn + ks))
        c = coefficients(
            base, ke, kw, kn, ks,
            spread(x[at_u]), spread(left[at_u]), spread(right[at_u]),
            spread(x[at_v]), spread(south[at_v]), spread(north[at_v]),
        )
        return stencil(c, x, left, right, south, north)

    def to_inner(row, value):
        picked = jnp.where(rows_of(flat) == lane_f // 4, take_lanes(value, column_f), 0.0)
        inner[pl.ds(row, 1), :] = jnp.sum(picked, axis=0, keepdims=True)

    def two_rows(buf, first):
        fields_of = buf[pl.ds(first, nplane), :]
        e_weight, n_weight, k = (buf[pl.ds(first + nplane + i, 1), :] for i in range(3))
        return fields_of, k, e_weight, n_weight

    x0, k0, e0, n0 = two_rows(send_s, 0)
    x1, k1, e1, n1 = two_rows(send_s, 28)
    y0, ky, ey, ny = two_rows(srows, 0)
    y1, _, _, ny1 = two_rows(srows, 28)
    out0 = row_step(y0, y1, x0, ky, ey, ny1, ny)
    in0 = row_step(x0, y0, x1, k0, e0, ny, n0)
    in1, in2 = edge_rows[0], edge_rows[1]
    to_inner(low_row, out0)
    to_inner(PAD, in0)
    south_0 = row_step(in0, out0, in1, k0, e0, ny, n0)
    south_1 = row_step(in1, in0, in2, k1, e1, n0, n1)

    x0, k0, e0, n0 = two_rows(send_n, 0)
    x1, k1, e1, n1 = two_rows(send_n, 28)
    n2 = weights[1, pl.ds(rows - 3, 1), :]
    y0, ky, ey, ny = two_rows(nrows, 0)
    y1, _, _, ny1 = two_rows(nrows, 28)
    ey = jnp.where(folded_1, roll(ey, -1, 1), ey)
    out0 = row_step(
        y0, x0, y1, ky, ey, jnp.where(folded_1, ny, n0), jnp.where(folded_1, ny1, ny)
    )
    in0 = row_step(x0, x1, y0, k0, e0, n1, n0)
    in1, in2 = edge_rows[2], edge_rows[3]
    to_inner(top_row, out0)
    to_inner(top_row - 1, in0)
    north_0 = row_step(in0, in1, out0, k0, e0, n1, n0)
    north_1 = row_step(in1, in2, in0, k1, e1, n2, n1)
    for i, value in enumerate((south_0, south_1, north_0, north_1)):
        edge_rows[i] = value
    for i, row in enumerate((0, 1, rows - 1, rows - 2)):
        for p in range(nplane):
            state[p, pl.ds(row, 1), :] = edge_rows[i, pl.ds(p, 1), :]

    arrived(recv_we.at[0], WEST)
    arrived(recv_we.at[1], EAST)

    @pl.when(not_bottom)
    def _():
        arrived(recv_c.at[0], SOUTHWEST)
        arrived(recv_c.at[1], SOUTHEAST)

    @pl.when(ne_other)
    def _():
        arrived(recv_c.at[3], NORTHEAST)

    @pl.when(nw_other)
    def _():
        arrived(recv_c.at[2], NORTHWEST)

    eight = (8, LANES)
    lane8 = lanes_of(eight)
    slot8 = lane8 % 4
    flip8 = jnp.where(jnp.logical_and(lane8 >= 16 * nlevel, lane8 < 4 * nplane), -1.0, 1.0)
    east8 = lane8 // 4 == nplane

    def beyond(block):
        upside = jnp.concatenate([block[7 - i : 8 - i, :] for i in range(8)], axis=0)
        mirrored = flip8 * take_lanes(upside, lane8 - slot8 + (3 - slot8))
        mirrored = jnp.where(east8, roll(mirrored, -1, 1), mirrored)
        return mirrored

    middle_n = recv_ns[1, pl.ds(56, 8), :]
    middle_s = recv_ns[0, pl.ds(56, 8), :]
    slot = lane_h % 4
    place = 2 * (lane_h // 4) + lane_h % 2
    for start in (0, half):
        piece = pl.ds(start, half)
        own, at = packed[piece, :], place + (64 if start else 0)
        strips[0, pl.ds(PAD + start, half), :] = jnp.where(slot < 2, take_lanes(recv_we[0], at), own)
        strips[1, pl.ds(PAD + start, half), :] = jnp.where(slot < 2, own, take_lanes(recv_we[1], at))
    strips[0, pl.ds(0, 8), :] = jnp.where(slot8 < 2, recv_c[0], middle_s)
    strips[1, pl.ds(0, 8), :] = jnp.where(slot8 < 2, middle_s, recv_c[1])
    for side in range(2):
        lower, upper = ((recv_c[2], middle_n), (middle_n, recv_c[3]))[side]
        strips[side, pl.ds(top_row, 8), :] = jnp.where(
            at_top(eight),
            beyond(jnp.where(slot8 >= 2, lower, upper)),
            jnp.where(slot8 < 2, lower, upper),
        )

    tall = (rows + 2 * PAD, LANES)
    slot_t = lanes_of(tall) % 4
    lane_t = lanes_of(tall)
    folded = jnp.logical_and(at_top(tall), rows_of(tall) == top_row)

    beyond_125 = take_lanes(weights[0], jnp.full((rows, LANES), LANES - 3, jnp.int32))
    beyond_125 = jnp.concatenate([beyond_125[:PAD], beyond_125, beyond_125[:PAD]], axis=0)
    inner_all = inner[...]
    index_u = 16 * nlevel + lane_t % (4 * nlevel)
    index_v = 20 * nlevel + lane_t % (4 * nlevel)

    def strip_step(w, x, left, right):
        south, north = roll(x, 1, 0), roll(x, -1, 0)
        u = take_lanes(x, index_u), take_lanes(left, index_u), take_lanes(right, index_u)
        v = take_lanes(x, index_v)
        c = coefficients(*w, *u, v, roll(v, 1, 0), roll(v, -1, 0))
        return stencil(c, x, left, right, south, north)

    advanced = []
    for side in range(2):
        x = strips[side]
        e_weight, n_weight, k = (
            take_lanes(x, 4 * (nplane + i) + slot_t) for i in range(3)
        )
        w_weight = jnp.where(slot_t == 0, beyond_125, roll(e_weight, 1, 1))
        n_south = jnp.where(folded, n_weight, roll(n_weight, 1, 0))
        n_north = jnp.where(folded, roll(n_weight, -1, 0), n_weight)
        ke, kw, kn, ks = k * e_weight, k * w_weight, k * n_north, k * n_south
        w = (1.0 - ((ke + kw) + (kn + ks)), ke, kw, kn, ks)
        x = strip_step(w, x, roll(x, 1, 1), roll(x, -1, 1))
        x = jnp.where(
            slot_t == 0, roll(inner_all, -1, 1), jnp.where(slot_t == 3, roll(inner_all, 1, 1), x)
        )
        left = jnp.where(slot_t == 0, inner_all, roll(x, 1, 1))
        right = jnp.where(slot_t == 3, inner_all, roll(x, -1, 1))
        advanced.append(strip_step(w, x, left, right))
    final = jnp.where(slot_t < 2, advanced[1], advanced[0])
    columns[...] = final[PAD : PAD + rows, :]

    go_w.wait_send()
    go_e.wait_send()
    go_n.wait_send()

    @pl.when(ne_other)
    def _():
        go_ne.wait_send()

    @pl.when(nw_other)
    def _():
        go_nw.wait_send()

    @pl.when(not_bottom)
    def _():
        go_s.wait_send()
        go_se.wait_send()
        go_sw.wait_send()


def second_kernel(state, columns, out, obuf, out_sems):
    nplane, rows, cols = state.shape
    lane = lanes_of((rows, cols))
    is_edge = jnp.logical_or(lane < 2, lane >= LANES - 2)
    parts = out_sems.shape[0]
    size = nplane // parts
    copies = []
    for part in range(parts):
        for p in range(part * size, (part + 1) * size):
            obuf[p] = jnp.where(is_edge, roll(columns[...], -(4 * p + 2), 1), state[p])
        piece = pl.ds(part * size, size)
        copies.append(pltpu.make_async_copy(obuf.at[piece], out.at[piece], out_sems.at[part]))
        copies[-1].start()
    for copy in copies:
        copy.wait()


def solution(mesh):
    nlon, nlat = mesh.shape["lon"], mesh.shape["lat"]

    def local(fields, face_weights, inv_area, cell_mask, land_blocks):
        nfield, nlevel, rows, cols = fields.shape
        nplane = nfield * nlevel
        tall = rows + 2 * PAD
        f32 = jnp.float32
        anywhere = pl.BlockSpec(memory_space=pl.ANY)
        near = pl.BlockSpec(memory_space=pltpu.VMEM)

        def far(value):
            return pltpu.with_memory_space_constraint(value, pltpu.HBM)

        def first(*refs):
            first_kernel(nlon, nlat, nfield, nlevel, *refs)

        def second(*refs):
            second_kernel(*refs)

        passed = pl.pallas_call(
            first,
            out_shape=[
                pltpu.VMEM((nplane, rows, cols), f32),
                pltpu.VMEM((rows, cols), f32),
            ],
            in_specs=[anywhere] * 4 + [pl.BlockSpec(memory_space=pltpu.SMEM)],
            out_specs=[near] * 2,
            scratch_shapes=[
                pltpu.VMEM((nplane, tall, cols), f32),
                pltpu.VMEM((nplane, tall, cols), f32),
                pltpu.VMEM((5, rows, cols), f32),
                pltpu.VMEM((2, rows, cols), f32),
                pltpu.VMEM((rows, cols), f32),
                pltpu.VMEM((rows, cols), jnp.int32),
                pltpu.VMEM((rows, cols), f32),
                pltpu.VMEM((rows, cols), f32),
                pltpu.VMEM((64, cols), f32),
                pltpu.VMEM((64, cols), f32),
                pltpu.VMEM((2, rows // 2, cols), f32),
                pltpu.VMEM((2, rows // 2, cols), f32),
                pltpu.VMEM((2, 64, cols), f32),
                pltpu.VMEM((4, 8, cols), f32),
                pltpu.VMEM((tall, cols), f32),
                pltpu.VMEM((2, tall, cols), f32),
                pltpu.VMEM((56, cols), f32),
                pltpu.VMEM((56, cols), f32),
                pltpu.VMEM((4, nplane, cols), f32),
                pltpu.SemaphoreType.DMA((3 + rows // CHUNK,)),
                pltpu.SemaphoreType.DMA((8,)),
                pltpu.SemaphoreType.DMA((8,)),
            ],
            compiler_params=pltpu.CompilerParams(
                collective_id=0, has_side_effects=True, vmem_limit_bytes=16 * 1024 * 1024
            ),
        )(
            far(fields.reshape(nplane, rows, cols)), far(face_weights), far(inv_area),
            far(cell_mask), land_blocks,
        )
        result = pl.pallas_call(
            second,
            out_shape=pltpu.HBM((nplane, rows, cols), f32),
            in_specs=[near] * 2,
            out_specs=anywhere,
            scratch_shapes=[
                pltpu.VMEM((nplane, rows, cols), f32),
                pltpu.SemaphoreType.DMA((8,)),
            ],
            compiler_params=pltpu.CompilerParams(vmem_limit_bytes=16 * 1024 * 1024),
        )(*(pltpu.with_memory_space_constraint(value, pltpu.VMEM) for value in passed))
        return result.reshape(fields.shape)

    in_specs = (
        P(None, None, "lat", "lon"),
        P(None, "lat", "lon"),
        P("lat", "lon"),
        P("lat", "lon"),
        P("lat", "lon"),
    )
    out_specs = P(None, None, "lat", "lon")
    return jax.shard_map(local, mesh=mesh, in_specs=in_specs, out_specs=out_specs, check_vma=False)
```

```python
import jax
import jax.numpy as jnp
from jax import lax
from jax.experimental import pallas as pl
from jax.experimental.pallas import tpu as pltpu
from jax.sharding import PartitionSpec as P

TIME_STEP = 0.1
PAD = 8
CHUNK = 32
LANES = 128
WEST, EAST, SOUTH, NORTH, SOUTHWEST, SOUTHEAST, NORTHWEST, NORTHEAST = range(8)


def lanes_of(shape):
    return lax.broadcasted_iota(jnp.int32, shape, len(shape) - 1)


def rows_of(shape):
    return lax.broadcasted_iota(jnp.int32, shape, len(shape) - 2)


def roll(value, shift, axis):
    return pltpu.roll(value, shift % value.shape[axis], axis)


def take_lanes(value, index):
    return jnp.take_along_axis(value, index, axis=1)


def stencil(c, x, left, right, south, north):
    c0, ce, cw, cn, cs = c
    return c0 * x + ce * right + cw * left + cn * north + cs * south


def coefficients(base, ke, kw, kn, ks, u, u_left, u_right, v, v_south, v_north):
    pe = ke * (0.125 * (u + u_right))
    pw = kw * (0.125 * (u + u_left))
    pn = kn * (0.125 * (v + v_north))
    ps = ks * (0.125 * (v + v_south))
    return base + ((pw - pe) + (ps - pn)), ke - pe, kw + pw, kn - pn, ks + ps


def advance(source, coef, nfield, nlevel, level, put):
    rows = coef.shape[1]
    for start in range(0, rows, CHUNK):
        piece = pl.ds(start, CHUNK)
        base, ke, kw, kn, ks = (coef[i, piece, :] for i in range(5))

        def centre(field):
            return source[field * nlevel + level, pl.ds(PAD + start, CHUNK), :]

        def columns_beside(x):
            return roll(x, 1, 1), roll(x, -1, 1)

        def rows_beside(field):
            return (
                source[field * nlevel + level, pl.ds(PAD + start - 1, CHUNK), :],
                source[field * nlevel + level, pl.ds(PAD + start + 1, CHUNK), :],
            )

        u, v = centre(4), centre(5)
        u_sides, v_sides = columns_beside(u), rows_beside(5)
        c = coefficients(base, ke, kw, kn, ks, u, *u_sides, v, *v_sides)
        for field in range(nfield):
            x = centre(field)
            left, right = u_sides if field == 4 else columns_beside(x)
            south, north = v_sides if field == 5 else rows_beside(field)
            put(field, start, stencil(c, x, left, right, south, north))


def first_kernel(
    nlon, nlat, nfield, nlevel,
    fields, face_weights, inv_area, cell_mask, land,
    state, columns,
    ext0, ext1, coef, weights, area, cells, scale, packed, send_s, send_n,
    send_we, recv_we, recv_ns, recv_c, inner, strips, nrows, srows, edge_rows,
    in_sems, send_sems, recv_sems,
):
    nplane = nfield * nlevel
    rows = ext0.shape[1] - 2 * PAD
    top_row, low_row = PAD + rows, PAD - 1
    lon, lat = lax.axis_index("lon"), lax.axis_index("lat")
    is_top = lat == nlat - 1
    is_bottom = lat == 0
    east, west = lax.rem(lon + 1, nlon), lax.rem(lon + nlon - 1, nlon)
    north_lat = jnp.where(is_top, lat, lat + 1)
    north_lon = jnp.where(is_top, nlon - 1 - lon, lon)
    ne_lon = jnp.where(is_top, lax.rem(2 * nlon - 2 - lon, nlon), east)
    nw_lon = jnp.where(is_top, lax.rem(nlon - lon, nlon), west)
    ne_self = jnp.logical_and(is_top, ne_lon == lon)
    nw_self = jnp.logical_and(is_top, nw_lon == lon)
    ne_other = jnp.logical_not(ne_self)
    nw_other = jnp.logical_not(nw_self)
    not_bottom = jnp.logical_not(is_bottom)

    barrier = pltpu.get_barrier_semaphore()

    def greet(to_lon, to_lat):
        pl.semaphore_signal(
            barrier, inc=1, device_id={"lon": to_lon, "lat": to_lat},
            device_id_type=pl.DeviceIdType.MESH,
        )

    greet(west, lat)
    greet(east, lat)
    greet(north_lon, north_lat)

    @pl.when(ne_other)
    def _():
        greet(ne_lon, north_lat)

    @pl.when(nw_other)
    def _():
        greet(nw_lon, north_lat)

    @pl.when(not_bottom)
    def _():
        greet(lon, lat - 1)
        greet(east, lat - 1)
        greet(west, lat - 1)

    starts = range(0, rows, CHUNK)
    loads = [
        pltpu.make_async_copy(face_weights, weights, in_sems.at[0]),
        pltpu.make_async_copy(inv_area, area, in_sems.at[1]),
        pltpu.make_async_copy(cell_mask, cells, in_sems.at[2]),
    ]
    pieces = [
        pltpu.make_async_copy(
            fields.at[:, pl.ds(start, CHUNK), :], ext0.at[:, pl.ds(PAD + start, CHUNK), :],
            in_sems.at[3 + i],
        )
        for i, start in enumerate(starts)
    ]
    for load in loads + pieces:
        load.start()
    for load in loads:
        load.wait()
    sea = (1 - land[0, 0]).astype(jnp.float32)
    scale[...] = (TIME_STEP * sea) * cells[...].astype(jnp.float32) * area[...]

    group = lanes_of((CHUNK, LANES)) // 4
    for start, load in zip(starts, pieces):
        piece = pl.ds(start, CHUNK)
        load.wait()
        gathered = jnp.zeros((CHUNK, LANES), jnp.float32)
        for p in range(nplane + 3):
            if p < nplane:
                plane = ext0[p, pl.ds(PAD + start, CHUNK), :]
            elif p < nplane + 2:
                plane = weights[p - nplane, piece, :]
            else:
                plane = scale[piece, :]
            gathered = jnp.where(group == p, roll(plane, 4 * p + 2, 1), gathered)
        packed[piece, :] = gathered
    half = rows // 2
    lane_h = lanes_of((half, LANES))
    pick = 4 * ((lane_h % 64) // 2) + lane_h % 2
    for side in range(2):
        send_we[side] = jnp.where(
            lane_h < 64,
            take_lanes(packed[pl.ds(0, half), :], pick + 2 * side),
            take_lanes(packed[pl.ds(half, half), :], pick + 2 * side),
        )
    def remote(src, dst, number, slot, to_lon, to_lat):
        return pltpu.make_async_remote_copy(
            src_ref=src, dst_ref=dst, send_sem=send_sems.at[number], recv_sem=recv_sems.at[slot],
            device_id={"lon": to_lon, "lat": to_lat}, device_id_type=pl.DeviceIdType.MESH,
        )

    corner_s, corner_n = send_s.at[pl.ds(56, 8), :], send_n.at[pl.ds(56, 8), :]
    go_w = remote(send_we.at[1], recv_we.at[1], 0, EAST, west, lat)
    go_e = remote(send_we.at[0], recv_we.at[0], 1, WEST, east, lat)
    go_n = remote(
        send_n, recv_ns.at[jnp.where(is_top, 1, 0)], 2,
        jnp.where(is_top, NORTH, SOUTH), north_lon, north_lat,
    )
    go_ne = remote(
        corner_n, recv_c.at[jnp.where(is_top, 3, 0)], 3,
        jnp.where(is_top, NORTHEAST, SOUTHWEST), ne_lon, north_lat,
    )
    go_nw = remote(
        corner_n, recv_c.at[jnp.where(is_top, 2, 1)], 4,
        jnp.where(is_top, NORTHWEST, SOUTHEAST), nw_lon, north_lat,
    )
    go_s = remote(send_s, recv_ns.at[1], 5, NORTH, lon, lat - 1)
    go_se = remote(corner_s, recv_c.at[2], 6, NORTHWEST, east, lat - 1)
    go_sw = remote(corner_s, recv_c.at[3], 7, NORTHEAST, west, lat - 1)

    greetings = 3 + jnp.where(ne_self, 0, 1) + jnp.where(nw_self, 0, 1) + jnp.where(is_bottom, 0, 3)
    pl.semaphore_wait(barrier, greetings)
    go_w.start()
    go_e.start()

    for buf, first, second, corner in ((send_s, 0, 1, 0), (send_n, rows - 1, rows - 2, rows - 8)):
        for at, row in ((0, first), (28, second)):
            for p in range(nplane):
                buf[pl.ds(at + p, 1), :] = ext0[p, pl.ds(PAD + row, 1), :]
            for i in range(2):
                buf[pl.ds(at + nplane + i, 1), :] = weights[i, pl.ds(row, 1), :]
            buf[pl.ds(at + nplane + 2, 1), :] = scale[pl.ds(row, 1), :]
            buf[pl.ds(at + nplane + 3, 1), :] = jnp.zeros((1, LANES), jnp.float32)
        buf[pl.ds(56, 8), :] = packed[pl.ds(corner, 8), :]
    go_n.start()

    @pl.when(ne_other)
    def _():
        go_ne.start()

    @pl.when(nw_other)
    def _():
        go_nw.start()

    @pl.when(not_bottom)
    def _():
        go_s.start()
        go_se.start()
        go_sw.start()

    @pl.when(ne_self)
    def _():
        recv_c[3] = send_n[pl.ds(56, 8), :]

    @pl.when(nw_self)
    def _():
        recv_c[2] = send_n[pl.ds(56, 8), :]

    @pl.when(is_bottom)
    def _():
        recv_ns[0] = jnp.zeros(recv_ns.shape[1:], jnp.float32)
        recv_c[0] = jnp.zeros(recv_c.shape[1:], jnp.float32)
        recv_c[1] = jnp.zeros(recv_c.shape[1:], jnp.float32)

    def set_coefficients(start):
        piece = pl.ds(start, CHUNK)
        k = scale[piece, :]
        e_weight = weights[0, piece, :]
        n_weight = weights[1, piece, :]
        w_weight = roll(e_weight, 1, 1)
        if start:
            s_weight = weights[1, pl.ds(start - 1, CHUNK), :]
        else:
            s_weight = roll(n_weight, 1, 0)
        ke, kw, kn, ks = k * e_weight, k * w_weight, k * n_weight, k * s_weight
        coef[0, piece, :] = 1.0 - ((ke + kw) + (kn + ks))
        coef[1, piece, :] = ke
        coef[2, piece, :] = kw
        coef[3, piece, :] = kn
        coef[4, piece, :] = ks

    for start in starts:
        set_coefficients(start)

    @pl.loop(0, nlevel)
    def _(level):
        def put(field, start, value):
            ext1[field * nlevel + level, pl.ds(PAD + start, CHUNK), :] = value

        advance(ext0, coef, nfield, nlevel, level, put)

    @pl.loop(0, nlevel)
    def _(level):
        def put(field, start, value):
            state[field * nlevel + level, pl.ds(start, CHUNK), :] = value

        advance(ext1, coef, nfield, nlevel, level, put)

    for start in range(0, rows + 2 * PAD, 48):
        piece = pl.ds(start, 48)
        lane = lanes_of((48, LANES))
        gathered = jnp.zeros((48, LANES), jnp.float32)
        for p in range(nplane):
            plane = ext1[p, piece, :]
            gathered = jnp.where(lane // 2 == 2 * p, roll(plane, 4 * p + 3, 1), gathered)
            gathered = jnp.where(lane // 2 == 2 * p + 1, roll(plane, 4 * p + 1, 1), gathered)
        inner[piece, :] = gathered

    for i, row in enumerate((PAD + 1, PAD + 2, top_row - 2, top_row - 3)):
        for p in range(nplane):
            edge_rows[i, pl.ds(p, 1), :] = ext1[p, pl.ds(row, 1), :]

    def arrived(dst, slot):
        remote(dst, dst, 0, slot, west, lat).wait_recv()

    arrived(recv_ns.at[1], NORTH)

    @pl.when(not_bottom)
    def _():
        arrived(recv_ns.at[0], SOUTH)

    def at_top(shape):
        return jnp.full(shape, lat, jnp.int32) == nlat - 1

    shape = (56, LANES)
    came = recv_ns[1, pl.ds(0, 56), :]
    sub = rows_of(shape) % 28
    flips = jnp.where(jnp.logical_and(sub >= 4 * nlevel, sub < nplane), -1.0, 1.0)
    nrows[...] = jnp.where(
        at_top(shape), flips * take_lanes(came, LANES - 1 - lanes_of(shape)), came
    )
    srows[...] = recv_ns[0, pl.ds(0, 56), :]

    at_u, at_v = slice(4 * nlevel, 5 * nlevel), slice(5 * nlevel, 6 * nlevel)
    folded_1 = at_top((1, LANES))
    flat = (nplane, LANES)
    lane_f = lanes_of(flat)
    slot_f = lane_f % 4
    column_f = jnp.where(slot_f < 2, LANES - 3 + slot_f, slot_f - 1)

    def spread(value):
        return jnp.concatenate([value] * nfield, axis=0)

    def row_step(x, south, north, k, e_weight, n_south, n_north):
        left, right = roll(x, 1, 1), roll(x, -1, 1)
        ke, kw = k * e_weight, k * roll(e_weight, 1, 1)
        kn, ks = k * n_north, k * n_south
        base = 1.0 - ((ke + kw) + (kn + ks))
        c = coefficients(
            base, ke, kw, kn, ks,
            spread(x[at_u]), spread(left[at_u]), spread(right[at_u]),
            spread(x[at_v]), spread(south[at_v]), spread(north[at_v]),
        )
        return stencil(c, x, left, right, south, north)

    def to_inner(row, value):
        picked = jnp.where(rows_of(flat) == lane_f // 4, take_lanes(value, column_f), 0.0)
        inner[pl.ds(row, 1), :] = jnp.sum(picked, axis=0, keepdims=True)

    def two_rows(buf, first):
        fields_of = buf[pl.ds(first, nplane), :]
        e_weight, n_weight, k = (buf[pl.ds(first + nplane + i, 1), :] for i in range(3))
        return fields_of, k, e_weight, n_weight

    x0, k0, e0, n0 = two_rows(send_s, 0)
    x1, k1, e1, n1 = two_rows(send_s, 28)
    y0, ky, ey, ny = two_rows(srows, 0)
    y1, _, _, ny1 = two_rows(srows, 28)
    out0 = row_step(y0, y1, x0, ky, ey, ny1, ny)
    in0 = row_step(x0, y0, x1, k0, e0, ny, n0)
    in1, in2 = edge_rows[0], edge_rows[1]
    to_inner(low_row, out0)
    to_inner(PAD, in0)
    south_0 = row_step(in0, out0, in1, k0, e0, ny, n0)
    south_1 = row_step(in1, in0, in2, k1, e1, n0, n1)

    x0, k0, e0, n0 = two_rows(send_n, 0)
    x1, k1, e1, n1 = two_rows(send_n, 28)
    n2 = weights[1, pl.ds(rows - 3, 1), :]
    y0, ky, ey, ny = two_rows(nrows, 0)
    y1, _, _, ny1 = two_rows(nrows, 28)
    ey = jnp.where(folded_1, roll(ey, -1, 1), ey)
    out0 = row_step(
        y0, x0, y1, ky, ey, jnp.where(folded_1, ny, n0), jnp.where(folded_1, ny1, ny)
    )
    in0 = row_step(x0, x1, y0, k0, e0, n1, n0)
    in1, in2 = edge_rows[2], edge_rows[3]
    to_inner(top_row, out0)
    to_inner(top_row - 1, in0)
    north_0 = row_step(in0, in1, out0, k0, e0, n1, n0)
    north_1 = row_step(in1, in2, in0, k1, e1, n2, n1)
    for i, value in enumerate((south_0, south_1, north_0, north_1)):
        edge_rows[i] = value
    for i, row in enumerate((0, 1, rows - 1, rows - 2)):
        for p in range(nplane):
            state[p, pl.ds(row, 1), :] = edge_rows[i, pl.ds(p, 1), :]

    eight = (8, LANES)
    lane8 = lanes_of(eight)
    slot8 = lane8 % 4
    flip8 = jnp.where(jnp.logical_and(lane8 >= 16 * nlevel, lane8 < 4 * nplane), -1.0, 1.0)
    east8 = lane8 // 4 == nplane

    def beyond(block):
        upside = jnp.concatenate([block[7 - i : 8 - i, :] for i in range(8)], axis=0)
        mirrored = flip8 * take_lanes(upside, lane8 - slot8 + (3 - slot8))
        mirrored = jnp.where(east8, roll(mirrored, -1, 1), mirrored)
        return mirrored

    tall = (rows + 2 * PAD, LANES)
    slot_t = lanes_of(tall) % 4
    lane_t = lanes_of(tall)
    folded = jnp.logical_and(at_top(tall), rows_of(tall) == top_row)

    beyond_125 = take_lanes(weights[0], jnp.full((rows, LANES), LANES - 3, jnp.int32))
    beyond_125 = jnp.concatenate([beyond_125[:PAD], beyond_125, beyond_125[:PAD]], axis=0)
    inner_all = inner[...]
    index_u = 16 * nlevel + lane_t % (4 * nlevel)
    index_v = 20 * nlevel + lane_t % (4 * nlevel)

    def strip_step(w, x, left, right):
        south, north = roll(x, 1, 0), roll(x, -1, 0)
        u = take_lanes(x, index_u), take_lanes(left, index_u), take_lanes(right, index_u)
        v = take_lanes(x, index_v)
        c = coefficients(*w, *u, v, roll(v, 1, 0), roll(v, -1, 0))
        return stencil(c, x, left, right, south, north)

    middle_n = recv_ns[1, pl.ds(56, 8), :]
    middle_s = recv_ns[0, pl.ds(56, 8), :]
    slot = lane_h % 4
    place = 2 * (lane_h // 4) + lane_h % 2

    for turn in range(2):
        side = jnp.where(lon == 0, 1 - turn, turn)
        corner_other = jnp.where(side == 0, nw_other.astype(jnp.int32), ne_other.astype(jnp.int32))
        arrived(recv_we.at[side], WEST + side)

        @pl.when(not_bottom)
        def _():
            arrived(recv_c.at[side], SOUTHWEST + side)

        @pl.when(corner_other == 1)
        def _():
            arrived(recv_c.at[2 + side], NORTHWEST + side)

        block = recv_we[side]
        for start in (0, half):
            at = place + (64 if start else 0)
            strips[side, pl.ds(PAD + start, half), :] = jnp.where(
                slot // 2 == side, take_lanes(block, at), packed[pl.ds(start, half), :]
            )
        strips[side, pl.ds(0, 8), :] = jnp.where(slot8 // 2 == side, recv_c[side], middle_s)
        corner = recv_c[2 + side]
        strips[side, pl.ds(top_row, 8), :] = jnp.where(
            at_top(eight),
            beyond(jnp.where(slot8 // 2 == 1 - side, corner, middle_n)),
            jnp.where(slot8 // 2 == side, corner, middle_n),
        )
        x = strips[side]
        e_weight, n_weight, k = (
            take_lanes(x, 4 * (nplane + i) + slot_t) for i in range(3)
        )
        w_weight = jnp.where(slot_t == 0, beyond_125, roll(e_weight, 1, 1))
        n_south = jnp.where(folded, n_weight, roll(n_weight, 1, 0))
        n_north = jnp.where(folded, roll(n_weight, -1, 0), n_weight)
        ke, kw, kn, ks = k * e_weight, k * w_weight, k * n_north, k * n_south
        w = (1.0 - ((ke + kw) + (kn + ks)), ke, kw, kn, ks)
        x = strip_step(w, x, roll(x, 1, 1), roll(x, -1, 1))
        x = jnp.where(
            slot_t == 0, roll(inner_all, -1, 1), jnp.where(slot_t == 3, roll(inner_all, 1, 1), x)
        )
        left = jnp.where(slot_t == 0, inner_all, roll(x, 1, 1))
        right = jnp.where(slot_t == 3, inner_all, roll(x, -1, 1))
        strips[side] = strip_step(w, x, left, right)
    final = jnp.where(slot_t < 2, strips[1], strips[0])
    columns[...] = final[PAD : PAD + rows, :]

    go_w.wait_send()
    go_e.wait_send()
    go_n.wait_send()

    @pl.when(ne_other)
    def _():
        go_ne.wait_send()

    @pl.when(nw_other)
    def _():
        go_nw.wait_send()

    @pl.when(not_bottom)
    def _():
        go_s.wait_send()
        go_se.wait_send()
        go_sw.wait_send()


def second_kernel(state, columns, out, obuf, out_sems):
    nplane, rows, cols = state.shape
    lane = lanes_of((rows, cols))
    is_edge = jnp.logical_or(lane < 2, lane >= LANES - 2)
    parts = out_sems.shape[0]
    size = nplane // parts
    copies = []
    for part in range(parts):
        for p in range(part * size, (part + 1) * size):
            obuf[p] = jnp.where(is_edge, roll(columns[...], -(4 * p + 2), 1), state[p])
        piece = pl.ds(part * size, size)
        copies.append(pltpu.make_async_copy(obuf.at[piece], out.at[piece], out_sems.at[part]))
        copies[-1].start()
    for copy in copies:
        copy.wait()


def solution(mesh):
    nlon, nlat = mesh.shape["lon"], mesh.shape["lat"]

    def local(fields, face_weights, inv_area, cell_mask, land_blocks):
        nfield, nlevel, rows, cols = fields.shape
        nplane = nfield * nlevel
        tall = rows + 2 * PAD
        f32 = jnp.float32
        anywhere = pl.BlockSpec(memory_space=pl.ANY)
        near = pl.BlockSpec(memory_space=pltpu.VMEM)

        def far(value):
            return pltpu.with_memory_space_constraint(value, pltpu.HBM)

        def first(*refs):
            first_kernel(nlon, nlat, nfield, nlevel, *refs)

        def second(*refs):
            second_kernel(*refs)

        passed = pl.pallas_call(
            first,
            out_shape=[
                pltpu.VMEM((nplane, rows, cols), f32),
                pltpu.VMEM((rows, cols), f32),
            ],
            in_specs=[anywhere] * 4 + [pl.BlockSpec(memory_space=pltpu.SMEM)],
            out_specs=[near] * 2,
            scratch_shapes=[
                pltpu.VMEM((nplane, tall, cols), f32),
                pltpu.VMEM((nplane, tall, cols), f32),
                pltpu.VMEM((5, rows, cols), f32),
                pltpu.VMEM((2, rows, cols), f32),
                pltpu.VMEM((rows, cols), f32),
                pltpu.VMEM((rows, cols), jnp.int32),
                pltpu.VMEM((rows, cols), f32),
                pltpu.VMEM((rows, cols), f32),
                pltpu.VMEM((64, cols), f32),
                pltpu.VMEM((64, cols), f32),
                pltpu.VMEM((2, rows // 2, cols), f32),
                pltpu.VMEM((2, rows // 2, cols), f32),
                pltpu.VMEM((2, 64, cols), f32),
                pltpu.VMEM((4, 8, cols), f32),
                pltpu.VMEM((tall, cols), f32),
                pltpu.VMEM((2, tall, cols), f32),
                pltpu.VMEM((56, cols), f32),
                pltpu.VMEM((56, cols), f32),
                pltpu.VMEM((4, nplane, cols), f32),
                pltpu.SemaphoreType.DMA((3 + rows // CHUNK,)),
                pltpu.SemaphoreType.DMA((8,)),
                pltpu.SemaphoreType.DMA((8,)),
            ],
            compiler_params=pltpu.CompilerParams(
                collective_id=0, has_side_effects=True, vmem_limit_bytes=16 * 1024 * 1024
            ),
        )(
            far(fields.reshape(nplane, rows, cols)), far(face_weights), far(inv_area),
            far(cell_mask), land_blocks,
        )
        result = pl.pallas_call(
            second,
            out_shape=pltpu.HBM((nplane, rows, cols), f32),
            in_specs=[near] * 2,
            out_specs=anywhere,
            scratch_shapes=[
                pltpu.VMEM((nplane, rows, cols), f32),
                pltpu.SemaphoreType.DMA((8,)),
            ],
            compiler_params=pltpu.CompilerParams(vmem_limit_bytes=16 * 1024 * 1024),
        )(*(pltpu.with_memory_space_constraint(value, pltpu.VMEM) for value in passed))
        return result.reshape(fields.shape)

    in_specs = (
        P(None, None, "lat", "lon"),
        P(None, "lat", "lon"),
        P("lat", "lon"),
        P("lat", "lon"),
        P("lat", "lon"),
    )
    out_specs = P(None, None, "lat", "lon")
    return jax.shard_map(local, mesh=mesh, in_specs=in_specs, out_specs=out_specs, check_vma=False)
```

```python
import jax
import jax.numpy as jnp
from jax import lax
from jax.experimental import pallas as pl
from jax.experimental.pallas import tpu as pltpu
from jax.sharding import PartitionSpec as P

TIME_STEP = 0.1
PAD = 8
CHUNK = 32
LANES = 128
WEST, EAST, SOUTH, NORTH, SOUTHWEST, SOUTHEAST, NORTHWEST, NORTHEAST = range(8)


def lanes_of(shape):
    return lax.broadcasted_iota(jnp.int32, shape, len(shape) - 1)


def rows_of(shape):
    return lax.broadcasted_iota(jnp.int32, shape, len(shape) - 2)


def roll(value, shift, axis):
    return pltpu.roll(value, shift % value.shape[axis], axis)


def take_lanes(value, index):
    return jnp.take_along_axis(value, index, axis=1)


def stencil(c, x, left, right, south, north):
    c0, ce, cw, cn, cs = c
    return c0 * x + ce * right + cw * left + cn * north + cs * south


def coefficients(base, ke, kw, kn, ks, u, u_left, u_right, v, v_south, v_north):
    pe = ke * (0.125 * (u + u_right))
    pw = kw * (0.125 * (u + u_left))
    pn = kn * (0.125 * (v + v_north))
    ps = ks * (0.125 * (v + v_south))
    return base + ((pw - pe) + (ps - pn)), ke - pe, kw + pw, kn - pn, ks + ps


def advance(source, coef, nfield, nlevel, level, put):
    rows = coef.shape[1]
    for start in range(0, rows, CHUNK):
        piece = pl.ds(start, CHUNK)
        base, ke, kw, kn, ks = (coef[i, piece, :] for i in range(5))

        def centre(field):
            return source[field * nlevel + level, pl.ds(PAD + start, CHUNK), :]

        def columns_beside(x):
            return roll(x, 1, 1), roll(x, -1, 1)

        def rows_beside(field):
            return (
                source[field * nlevel + level, pl.ds(PAD + start - 1, CHUNK), :],
                source[field * nlevel + level, pl.ds(PAD + start + 1, CHUNK), :],
            )

        u, v = centre(4), centre(5)
        u_sides, v_sides = columns_beside(u), rows_beside(5)
        c = coefficients(base, ke, kw, kn, ks, u, *u_sides, v, *v_sides)
        for field in range(nfield):
            x = centre(field)
            left, right = u_sides if field == 4 else columns_beside(x)
            south, north = v_sides if field == 5 else rows_beside(field)
            put(field, start, stencil(c, x, left, right, south, north))


def first_kernel(
    nlon, nlat, nfield, nlevel,
    fields, face_weights, inv_area, cell_mask, land,
    state, columns,
    ext0, ext1, coef, weights, area, cells, scale, packed, send_s, send_n,
    send_we, recv_we, recv_ns, recv_c, inner, strips, nrows, srows, edge_rows,
    in_sems, send_sems, recv_sems,
):
    nplane = nfield * nlevel
    rows = ext0.shape[1] - 2 * PAD
    top_row, low_row = PAD + rows, PAD - 1
    lon, lat = lax.axis_index("lon"), lax.axis_index("lat")
    is_top = lat == nlat - 1
    is_bottom = lat == 0
    east, west = lax.rem(lon + 1, nlon), lax.rem(lon + nlon - 1, nlon)
    north_lat = jnp.where(is_top, lat, lat + 1)
    north_lon = jnp.where(is_top, nlon - 1 - lon, lon)
    ne_lon = jnp.where(is_top, lax.rem(2 * nlon - 2 - lon, nlon), east)
    nw_lon = jnp.where(is_top, lax.rem(nlon - lon, nlon), west)
    ne_self = jnp.logical_and(is_top, ne_lon == lon)
    nw_self = jnp.logical_and(is_top, nw_lon == lon)
    ne_other = jnp.logical_not(ne_self)
    nw_other = jnp.logical_not(nw_self)
    not_bottom = jnp.logical_not(is_bottom)

    barrier = pltpu.get_barrier_semaphore()

    def greet(to_lon, to_lat):
        pl.semaphore_signal(
            barrier, inc=1, device_id={"lon": to_lon, "lat": to_lat},
            device_id_type=pl.DeviceIdType.MESH,
        )

    greet(west, lat)
    greet(east, lat)
    greet(north_lon, north_lat)

    @pl.when(ne_other)
    def _():
        greet(ne_lon, north_lat)

    @pl.when(nw_other)
    def _():
        greet(nw_lon, north_lat)

    @pl.when(not_bottom)
    def _():
        greet(lon, lat - 1)
        greet(east, lat - 1)
        greet(west, lat - 1)

    starts = range(0, rows, CHUNK)
    loads = [
        pltpu.make_async_copy(face_weights, weights, in_sems.at[0]),
        pltpu.make_async_copy(inv_area, area, in_sems.at[1]),
        pltpu.make_async_copy(cell_mask, cells, in_sems.at[2]),
    ]
    pieces = [
        pltpu.make_async_copy(
            fields.at[:, pl.ds(start, CHUNK), :], ext0.at[:, pl.ds(PAD + start, CHUNK), :],
            in_sems.at[3 + i],
        )
        for i, start in enumerate(starts)
    ]
    for load in loads + pieces:
        load.start()
    for load in loads:
        load.wait()
    sea = (1 - land[0, 0]).astype(jnp.float32)
    scale[...] = (TIME_STEP * sea) * cells[...].astype(jnp.float32) * area[...]

    group = lanes_of((CHUNK, LANES)) // 4
    for start, load in zip(starts, pieces):
        piece = pl.ds(start, CHUNK)
        load.wait()
        gathered = jnp.zeros((CHUNK, LANES), jnp.float32)
        for p in range(nplane + 3):
            if p < nplane:
                plane = ext0[p, pl.ds(PAD + start, CHUNK), :]
            elif p < nplane + 2:
                plane = weights[p - nplane, piece, :]
            else:
                plane = scale[piece, :]
            gathered = jnp.where(group == p, roll(plane, 4 * p + 2, 1), gathered)
        packed[piece, :] = gathered
    half = rows // 2
    lane_h = lanes_of((half, LANES))
    pick = 4 * ((lane_h % 64) // 2) + lane_h % 2
    for side in range(2):
        send_we[side] = jnp.where(
            lane_h < 64,
            take_lanes(packed[pl.ds(0, half), :], pick + 2 * side),
            take_lanes(packed[pl.ds(half, half), :], pick + 2 * side),
        )
    def remote(src, dst, number, slot, to_lon, to_lat):
        return pltpu.make_async_remote_copy(
            src_ref=src, dst_ref=dst, send_sem=send_sems.at[number], recv_sem=recv_sems.at[slot],
            device_id={"lon": to_lon, "lat": to_lat}, device_id_type=pl.DeviceIdType.MESH,
        )

    corner_s, corner_n = packed.at[pl.ds(0, 8), :], packed.at[pl.ds(rows - 8, 8), :]
    go_w = remote(send_we.at[1], recv_we.at[1], 0, EAST, west, lat)
    go_e = remote(send_we.at[0], recv_we.at[0], 1, WEST, east, lat)
    go_n = remote(
        send_n, recv_ns.at[jnp.where(is_top, 1, 0)], 2,
        jnp.where(is_top, NORTH, SOUTH), north_lon, north_lat,
    )
    go_ne = remote(
        corner_n, recv_c.at[jnp.where(is_top, 3, 0)], 3,
        jnp.where(is_top, NORTHEAST, SOUTHWEST), ne_lon, north_lat,
    )
    go_nw = remote(
        corner_n, recv_c.at[jnp.where(is_top, 2, 1)], 4,
        jnp.where(is_top, NORTHWEST, SOUTHEAST), nw_lon, north_lat,
    )
    go_s = remote(send_s, recv_ns.at[1], 5, NORTH, lon, lat - 1)
    go_se = remote(corner_s, recv_c.at[2], 6, NORTHWEST, east, lat - 1)
    go_sw = remote(corner_s, recv_c.at[3], 7, NORTHEAST, west, lat - 1)

    def set_coefficients(start):
        piece = pl.ds(start, CHUNK)
        k = scale[piece, :]
        e_weight = weights[0, piece, :]
        n_weight = weights[1, piece, :]
        w_weight = roll(e_weight, 1, 1)
        if start:
            s_weight = weights[1, pl.ds(start - 1, CHUNK), :]
        else:
            s_weight = roll(n_weight, 1, 0)
        ke, kw, kn, ks = k * e_weight, k * w_weight, k * n_weight, k * s_weight
        coef[0, piece, :] = 1.0 - ((ke + kw) + (kn + ks))
        coef[1, piece, :] = ke
        coef[2, piece, :] = kw
        coef[3, piece, :] = kn
        coef[4, piece, :] = ks

    def advance_block():
        for start in starts:
            set_coefficients(start)

        @pl.loop(0, nlevel)
        def _(level):
            def put(field, start, value):
                ext1[field * nlevel + level, pl.ds(PAD + start, CHUNK), :] = value

            advance(ext0, coef, nfield, nlevel, level, put)

        @pl.loop(0, nlevel)
        def _(level):
            def put(field, start, value):
                state[field * nlevel + level, pl.ds(start, CHUNK), :] = value

            advance(ext1, coef, nfield, nlevel, level, put)

        for start in range(0, rows + 2 * PAD, 48):
            piece = pl.ds(start, 48)
            lane = lanes_of((48, LANES))
            gathered = jnp.zeros((48, LANES), jnp.float32)
            for p in range(nplane):
                plane = ext1[p, piece, :]
                gathered = jnp.where(lane // 2 == 2 * p, roll(plane, 4 * p + 3, 1), gathered)
                gathered = jnp.where(lane // 2 == 2 * p + 1, roll(plane, 4 * p + 1, 1), gathered)
            inner[piece, :] = gathered

        for i, row in enumerate((PAD + 1, PAD + 2, top_row - 2, top_row - 3)):
            for p in range(nplane):
                edge_rows[i, pl.ds(p, 1), :] = ext1[p, pl.ds(row, 1), :]

    @pl.when(lon == 0)
    def _():
        advance_block()

    greetings = 3 + jnp.where(ne_self, 0, 1) + jnp.where(nw_self, 0, 1) + jnp.where(is_bottom, 0, 3)
    pl.semaphore_wait(barrier, greetings)

    @pl.when(ne_other)
    def _():
        go_ne.start()

    @pl.when(nw_other)
    def _():
        go_nw.start()

    @pl.when(not_bottom)
    def _():
        go_se.start()
        go_sw.start()

    go_w.start()
    go_e.start()

    for buf, first, second, corner in ((send_s, 0, 1, 0), (send_n, rows - 1, rows - 2, rows - 8)):
        for at, row in ((0, first), (28, second)):
            for p in range(nplane):
                buf[pl.ds(at + p, 1), :] = ext0[p, pl.ds(PAD + row, 1), :]
            for i in range(2):
                buf[pl.ds(at + nplane + i, 1), :] = weights[i, pl.ds(row, 1), :]
            buf[pl.ds(at + nplane + 2, 1), :] = scale[pl.ds(row, 1), :]
            buf[pl.ds(at + nplane + 3, 1), :] = jnp.zeros((1, LANES), jnp.float32)
        buf[pl.ds(56, 8), :] = packed[pl.ds(corner, 8), :]
    go_n.start()

    @pl.when(not_bottom)
    def _():
        go_s.start()

    @pl.when(ne_self)
    def _():
        recv_c[3] = packed[pl.ds(rows - 8, 8), :]

    @pl.when(nw_self)
    def _():
        recv_c[2] = packed[pl.ds(rows - 8, 8), :]

    @pl.when(is_bottom)
    def _():
        recv_ns[0] = jnp.zeros(recv_ns.shape[1:], jnp.float32)
        recv_c[0] = jnp.zeros(recv_c.shape[1:], jnp.float32)
        recv_c[1] = jnp.zeros(recv_c.shape[1:], jnp.float32)

    @pl.when(lon != 0)
    def _():
        advance_block()

    def arrived(dst, slot):
        remote(dst, dst, 0, slot, west, lat).wait_recv()

    arrived(recv_ns.at[1], NORTH)

    @pl.when(not_bottom)
    def _():
        arrived(recv_ns.at[0], SOUTH)

    def at_top(shape):
        return jnp.full(shape, lat, jnp.int32) == nlat - 1

    shape = (56, LANES)
    came = recv_ns[1, pl.ds(0, 56), :]
    sub = rows_of(shape) % 28
    flips = jnp.where(jnp.logical_and(sub >= 4 * nlevel, sub < nplane), -1.0, 1.0)
    nrows[...] = jnp.where(
        at_top(shape), flips * take_lanes(came, LANES - 1 - lanes_of(shape)), came
    )
    srows[...] = recv_ns[0, pl.ds(0, 56), :]

    at_u, at_v = slice(4 * nlevel, 5 * nlevel), slice(5 * nlevel, 6 * nlevel)
    folded_1 = at_top((1, LANES))
    flat = (nplane, LANES)
    lane_f = lanes_of(flat)
    slot_f = lane_f % 4
    column_f = jnp.where(slot_f < 2, LANES - 3 + slot_f, slot_f - 1)

    def spread(value):
        return jnp.concatenate([value] * nfield, axis=0)

    def row_step(x, south, north, k, e_weight, n_south, n_north):
        left, right = roll(x, 1, 1), roll(x, -1, 1)
        ke, kw = k * e_weight, k * roll(e_weight, 1, 1)
        kn, ks = k * n_north, k * n_south
        base = 1.0 - ((ke + kw) + (kn + ks))
        c = coefficients(
            base, ke, kw, kn, ks,
            spread(x[at_u]), spread(left[at_u]), spread(right[at_u]),
            spread(x[at_v]), spread(south[at_v]), spread(north[at_v]),
        )
        return stencil(c, x, left, right, south, north)

    def to_inner(row, value):
        picked = jnp.where(rows_of(flat) == lane_f // 4, take_lanes(value, column_f), 0.0)
        inner[pl.ds(row, 1), :] = jnp.sum(picked, axis=0, keepdims=True)

    def two_rows(buf, first):
        fields_of = buf[pl.ds(first, nplane), :]
        e_weight, n_weight, k = (buf[pl.ds(first + nplane + i, 1), :] for i in range(3))
        return fields_of, k, e_weight, n_weight

    x0, k0, e0, n0 = two_rows(send_s, 0)
    x1, k1, e1, n1 = two_rows(send_s, 28)
    y0, ky, ey, ny = two_rows(srows, 0)
    y1, _, _, ny1 = two_rows(srows, 28)
    out0 = row_step(y0, y1, x0, ky, ey, ny1, ny)
    in0 = row_step(x0, y0, x1, k0, e0, ny, n0)
    in1, in2 = edge_rows[0], edge_rows[1]
    to_inner(low_row, out0)
    to_inner(PAD, in0)
    south_0 = row_step(in0, out0, in1, k0, e0, ny, n0)
    south_1 = row_step(in1, in0, in2, k1, e1, n0, n1)

    x0, k0, e0, n0 = two_rows(send_n, 0)
    x1, k1, e1, n1 = two_rows(send_n, 28)
    n2 = weights[1, pl.ds(rows - 3, 1), :]
    y0, ky, ey, ny = two_rows(nrows, 0)
    y1, _, _, ny1 = two_rows(nrows, 28)
    ey = jnp.where(folded_1, roll(ey, -1, 1), ey)
    out0 = row_step(
        y0, x0, y1, ky, ey, jnp.where(folded_1, ny, n0), jnp.where(folded_1, ny1, ny)
    )
    in0 = row_step(x0, x1, y0, k0, e0, n1, n0)
    in1, in2 = edge_rows[2], edge_rows[3]
    to_inner(top_row, out0)
    to_inner(top_row - 1, in0)
    north_0 = row_step(in0, in1, out0, k0, e0, n1, n0)
    north_1 = row_step(in1, in2, in0, k1, e1, n2, n1)
    for i, value in enumerate((south_0, south_1, north_0, north_1)):
        edge_rows[i] = value
    for i, row in enumerate((0, 1, rows - 1, rows - 2)):
        for p in range(nplane):
            state[p, pl.ds(row, 1), :] = edge_rows[i, pl.ds(p, 1), :]

    eight = (8, LANES)
    lane8 = lanes_of(eight)
    slot8 = lane8 % 4
    flip8 = jnp.where(jnp.logical_and(lane8 >= 16 * nlevel, lane8 < 4 * nplane), -1.0, 1.0)
    east8 = lane8 // 4 == nplane

    def beyond(block):
        upside = jnp.concatenate([block[7 - i : 8 - i, :] for i in range(8)], axis=0)
        mirrored = flip8 * take_lanes(upside, lane8 - slot8 + (3 - slot8))
        mirrored = jnp.where(east8, roll(mirrored, -1, 1), mirrored)
        return mirrored

    tall = (rows + 2 * PAD, LANES)
    slot_t = lanes_of(tall) % 4
    lane_t = lanes_of(tall)
    folded = jnp.logical_and(at_top(tall), rows_of(tall) == top_row)

    beyond_125 = take_lanes(weights[0], jnp.full((rows, LANES), LANES - 3, jnp.int32))
    beyond_125 = jnp.concatenate([beyond_125[:PAD], beyond_125, beyond_125[:PAD]], axis=0)
    inner_all = inner[...]
    index_u = 16 * nlevel + lane_t % (4 * nlevel)
    index_v = 20 * nlevel + lane_t % (4 * nlevel)

    def strip_step(w, x, left, right):
        south, north = roll(x, 1, 0), roll(x, -1, 0)
        u = take_lanes(x, index_u), take_lanes(left, index_u), take_lanes(right, index_u)
        v = take_lanes(x, index_v)
        c = coefficients(*w, *u, v, roll(v, 1, 0), roll(v, -1, 0))
        return stencil(c, x, left, right, south, north)

    middle_n = recv_ns[1, pl.ds(56, 8), :]
    middle_s = recv_ns[0, pl.ds(56, 8), :]
    slot = lane_h % 4
    place = 2 * (lane_h // 4) + lane_h % 2

    for turn in range(2):
        side = jnp.where(lon == 0, 1 - turn, turn)
        corner_other = jnp.where(side == 0, nw_other.astype(jnp.int32), ne_other.astype(jnp.int32))
        arrived(recv_we.at[side], WEST + side)

        @pl.when(not_bottom)
        def _():
            arrived(recv_c.at[side], SOUTHWEST + side)

        @pl.when(corner_other == 1)
        def _():
            arrived(recv_c.at[2 + side], NORTHWEST + side)

        block = recv_we[side]
        for start in (0, half):
            at = place + (64 if start else 0)
            strips[side, pl.ds(PAD + start, half), :] = jnp.where(
                slot // 2 == side, take_lanes(block, at), packed[pl.ds(start, half), :]
            )
        strips[side, pl.ds(0, 8), :] = jnp.where(slot8 // 2 == side, recv_c[side], middle_s)
        corner = recv_c[2 + side]
        strips[side, pl.ds(top_row, 8), :] = jnp.where(
            at_top(eight),
            beyond(jnp.where(slot8 // 2 == 1 - side, corner, middle_n)),
            jnp.where(slot8 // 2 == side, corner, middle_n),
        )
        x = strips[side]
        e_weight, n_weight, k = (
            take_lanes(x, 4 * (nplane + i) + slot_t) for i in range(3)
        )
        w_weight = jnp.where(slot_t == 0, beyond_125, roll(e_weight, 1, 1))
        n_south = jnp.where(folded, n_weight, roll(n_weight, 1, 0))
        n_north = jnp.where(folded, roll(n_weight, -1, 0), n_weight)
        ke, kw, kn, ks = k * e_weight, k * w_weight, k * n_north, k * n_south
        w = (1.0 - ((ke + kw) + (kn + ks)), ke, kw, kn, ks)
        x = strip_step(w, x, roll(x, 1, 1), roll(x, -1, 1))
        x = jnp.where(
            slot_t == 0, roll(inner_all, -1, 1), jnp.where(slot_t == 3, roll(inner_all, 1, 1), x)
        )
        left = jnp.where(slot_t == 0, inner_all, roll(x, 1, 1))
        right = jnp.where(slot_t == 3, inner_all, roll(x, -1, 1))
        strips[side] = strip_step(w, x, left, right)
    final = jnp.where(slot_t < 2, strips[1], strips[0])
    columns[...] = final[PAD : PAD + rows, :]

    go_w.wait_send()
    go_e.wait_send()
    go_n.wait_send()

    @pl.when(ne_other)
    def _():
        go_ne.wait_send()

    @pl.when(nw_other)
    def _():
        go_nw.wait_send()

    @pl.when(not_bottom)
    def _():
        go_s.wait_send()
        go_se.wait_send()
        go_sw.wait_send()


def second_kernel(state, columns, out, obuf, out_sems):
    nplane, rows, cols = state.shape
    lane = lanes_of((rows, cols))
    is_edge = jnp.logical_or(lane < 2, lane >= LANES - 2)
    parts = out_sems.shape[0]
    size = nplane // parts
    copies = []
    for part in range(parts):
        for p in range(part * size, (part + 1) * size):
            obuf[p] = jnp.where(is_edge, roll(columns[...], -(4 * p + 2), 1), state[p])
        piece = pl.ds(part * size, size)
        copies.append(pltpu.make_async_copy(obuf.at[piece], out.at[piece], out_sems.at[part]))
        copies[-1].start()
    for copy in copies:
        copy.wait()


def solution(mesh):
    nlon, nlat = mesh.shape["lon"], mesh.shape["lat"]

    def local(fields, face_weights, inv_area, cell_mask, land_blocks):
        nfield, nlevel, rows, cols = fields.shape
        nplane = nfield * nlevel
        tall = rows + 2 * PAD
        f32 = jnp.float32
        anywhere = pl.BlockSpec(memory_space=pl.ANY)
        near = pl.BlockSpec(memory_space=pltpu.VMEM)

        def far(value):
            return pltpu.with_memory_space_constraint(value, pltpu.HBM)

        def first(*refs):
            first_kernel(nlon, nlat, nfield, nlevel, *refs)

        def second(*refs):
            second_kernel(*refs)

        passed = pl.pallas_call(
            first,
            out_shape=[
                pltpu.VMEM((nplane, rows, cols), f32),
                pltpu.VMEM((rows, cols), f32),
            ],
            in_specs=[anywhere] * 4 + [pl.BlockSpec(memory_space=pltpu.SMEM)],
            out_specs=[near] * 2,
            scratch_shapes=[
                pltpu.VMEM((nplane, tall, cols), f32),
                pltpu.VMEM((nplane, tall, cols), f32),
                pltpu.VMEM((5, rows, cols), f32),
                pltpu.VMEM((2, rows, cols), f32),
                pltpu.VMEM((rows, cols), f32),
                pltpu.VMEM((rows, cols), jnp.int32),
                pltpu.VMEM((rows, cols), f32),
                pltpu.VMEM((rows, cols), f32),
                pltpu.VMEM((64, cols), f32),
                pltpu.VMEM((64, cols), f32),
                pltpu.VMEM((2, rows // 2, cols), f32),
                pltpu.VMEM((2, rows // 2, cols), f32),
                pltpu.VMEM((2, 64, cols), f32),
                pltpu.VMEM((4, 8, cols), f32),
                pltpu.VMEM((tall, cols), f32),
                pltpu.VMEM((2, tall, cols), f32),
                pltpu.VMEM((56, cols), f32),
                pltpu.VMEM((56, cols), f32),
                pltpu.VMEM((4, nplane, cols), f32),
                pltpu.SemaphoreType.DMA((3 + rows // CHUNK,)),
                pltpu.SemaphoreType.DMA((8,)),
                pltpu.SemaphoreType.DMA((8,)),
            ],
            compiler_params=pltpu.CompilerParams(
                collective_id=0, has_side_effects=True, vmem_limit_bytes=16 * 1024 * 1024
            ),
        )(
            far(fields.reshape(nplane, rows, cols)), far(face_weights), far(inv_area),
            far(cell_mask), land_blocks,
        )
        result = pl.pallas_call(
            second,
            out_shape=pltpu.HBM((nplane, rows, cols), f32),
            in_specs=[near] * 2,
            out_specs=anywhere,
            scratch_shapes=[
                pltpu.VMEM((nplane, rows, cols), f32),
                pltpu.SemaphoreType.DMA((8,)),
            ],
            compiler_params=pltpu.CompilerParams(vmem_limit_bytes=16 * 1024 * 1024),
        )(*(pltpu.with_memory_space_constraint(value, pltpu.VMEM) for value in passed))
        return result.reshape(fields.shape)

    in_specs = (
        P(None, None, "lat", "lon"),
        P(None, "lat", "lon"),
        P("lat", "lon"),
        P("lat", "lon"),
        P("lat", "lon"),
    )
    out_specs = P(None, None, "lat", "lon")
    return jax.shard_map(local, mesh=mesh, in_specs=in_specs, out_specs=out_specs, check_vma=False)
```

```python
import jax
import jax.numpy as jnp
from jax import lax
from jax.experimental import pallas as pl
from jax.experimental.pallas import tpu as pltpu
from jax.sharding import PartitionSpec as P

TIME_STEP = 0.1
PAD = 8
CHUNK = 32
LANES = 128
WEST, EAST, SOUTH, NORTH, SOUTHWEST, SOUTHEAST, NORTHWEST, NORTHEAST = range(8)


def lanes_of(shape):
    return lax.broadcasted_iota(jnp.int32, shape, len(shape) - 1)


def rows_of(shape):
    return lax.broadcasted_iota(jnp.int32, shape, len(shape) - 2)


def roll(value, shift, axis):
    return pltpu.roll(value, shift % value.shape[axis], axis)


def take_lanes(value, index):
    return jnp.take_along_axis(value, index, axis=1)


def stencil(c, x, left, right, south, north):
    c0, ce, cw, cn, cs = c
    return c0 * x + ce * right + cw * left + cn * north + cs * south


def coefficients(base, ke, kw, kn, ks, u, u_left, u_right, v, v_south, v_north):
    pe = ke * (0.125 * (u + u_right))
    pw = kw * (0.125 * (u + u_left))
    pn = kn * (0.125 * (v + v_north))
    ps = ks * (0.125 * (v + v_south))
    return base + ((pw - pe) + (ps - pn)), ke - pe, kw + pw, kn - pn, ks + ps


def advance(source, coef, nfield, nlevel, level, put):
    rows = coef.shape[1]
    for start in range(0, rows, CHUNK):
        piece = pl.ds(start, CHUNK)
        base, ke, kw, kn, ks = (coef[i, piece, :] for i in range(5))

        def centre(field):
            return source[field * nlevel + level, pl.ds(PAD + start, CHUNK), :]

        def columns_beside(x):
            return roll(x, 1, 1), roll(x, -1, 1)

        def rows_beside(field):
            return (
                source[field * nlevel + level, pl.ds(PAD + start - 1, CHUNK), :],
                source[field * nlevel + level, pl.ds(PAD + start + 1, CHUNK), :],
            )

        u, v = centre(4), centre(5)
        u_sides, v_sides = columns_beside(u), rows_beside(5)
        c = coefficients(base, ke, kw, kn, ks, u, *u_sides, v, *v_sides)
        for field in range(nfield):
            x = centre(field)
            left, right = u_sides if field == 4 else columns_beside(x)
            south, north = v_sides if field == 5 else rows_beside(field)
            put(field, start, stencil(c, x, left, right, south, north))


def first_kernel(
    nlon, nlat, nfield, nlevel,
    fields, face_weights, inv_area, cell_mask, land,
    state, columns,
    ext0, ext1, coef, weights, area, cells, scale, packed, send_s, send_n,
    send_we, recv_we, recv_ns, recv_c, inner, strips, nrows, srows, edge_rows,
    in_sems, send_sems, recv_sems,
):
    nplane = nfield * nlevel
    rows = ext0.shape[1] - 2 * PAD
    top_row, low_row = PAD + rows, PAD - 1
    lon, lat = lax.axis_index("lon"), lax.axis_index("lat")
    is_top = lat == nlat - 1
    is_bottom = lat == 0
    east, west = lax.rem(lon + 1, nlon), lax.rem(lon + nlon - 1, nlon)
    north_lat = jnp.where(is_top, lat, lat + 1)
    north_lon = jnp.where(is_top, nlon - 1 - lon, lon)
    ne_lon = jnp.where(is_top, lax.rem(2 * nlon - 2 - lon, nlon), east)
    nw_lon = jnp.where(is_top, lax.rem(nlon - lon, nlon), west)
    ne_self = jnp.logical_and(is_top, ne_lon == lon)
    nw_self = jnp.logical_and(is_top, nw_lon == lon)
    ne_other = jnp.logical_not(ne_self)
    nw_other = jnp.logical_not(nw_self)
    not_bottom = jnp.logical_not(is_bottom)

    barrier = pltpu.get_barrier_semaphore()

    def greet(to_lon, to_lat):
        pl.semaphore_signal(
            barrier, inc=1, device_id={"lon": to_lon, "lat": to_lat},
            device_id_type=pl.DeviceIdType.MESH,
        )

    greet(west, lat)
    greet(east, lat)
    greet(north_lon, north_lat)

    @pl.when(ne_other)
    def _():
        greet(ne_lon, north_lat)

    @pl.when(nw_other)
    def _():
        greet(nw_lon, north_lat)

    @pl.when(not_bottom)
    def _():
        greet(lon, lat - 1)
        greet(east, lat - 1)
        greet(west, lat - 1)

    starts = range(0, rows, CHUNK)
    loads = [
        pltpu.make_async_copy(face_weights, weights, in_sems.at[0]),
        pltpu.make_async_copy(inv_area, area, in_sems.at[1]),
        pltpu.make_async_copy(cell_mask, cells, in_sems.at[2]),
    ]
    pieces = [
        pltpu.make_async_copy(
            fields.at[:, pl.ds(start, CHUNK), :], ext0.at[:, pl.ds(PAD + start, CHUNK), :],
            in_sems.at[3 + i],
        )
        for i, start in enumerate(starts)
    ]
    for load in loads + pieces:
        load.start()
    for load in loads:
        load.wait()
    sea = (1 - land[0, 0]).astype(jnp.float32)
    scale[...] = (TIME_STEP * sea) * cells[...].astype(jnp.float32) * area[...]

    group = lanes_of((CHUNK, LANES)) // 4
    for start, load in zip(starts, pieces):
        piece = pl.ds(start, CHUNK)
        load.wait()
        gathered = jnp.zeros((CHUNK, LANES), jnp.float32)
        for p in range(nplane + 3):
            if p < nplane:
                plane = ext0[p, pl.ds(PAD + start, CHUNK), :]
            elif p < nplane + 2:
                plane = weights[p - nplane, piece, :]
            else:
                plane = scale[piece, :]
            gathered = jnp.where(group == p, roll(plane, 4 * p + 2, 1), gathered)
        packed[piece, :] = gathered
    half = rows // 2
    lane_h = lanes_of((half, LANES))
    pick = 4 * ((lane_h % 64) // 2) + lane_h % 2
    for side in range(2):
        send_we[side] = jnp.where(
            lane_h < 64,
            take_lanes(packed[pl.ds(0, half), :], pick + 2 * side),
            take_lanes(packed[pl.ds(half, half), :], pick + 2 * side),
        )
    def remote(src, dst, number, slot, to_lon, to_lat):
        return pltpu.make_async_remote_copy(
            src_ref=src, dst_ref=dst, send_sem=send_sems.at[number], recv_sem=recv_sems.at[slot],
            device_id={"lon": to_lon, "lat": to_lat}, device_id_type=pl.DeviceIdType.MESH,
        )

    corner_s, corner_n = packed.at[pl.ds(0, 8), :], packed.at[pl.ds(rows - 8, 8), :]
    go_w = remote(send_we.at[1], recv_we.at[1], 0, EAST, west, lat)
    go_e = remote(send_we.at[0], recv_we.at[0], 1, WEST, east, lat)
    go_n = remote(
        send_n, recv_ns.at[jnp.where(is_top, 1, 0)], 2,
        jnp.where(is_top, NORTH, SOUTH), north_lon, north_lat,
    )
    go_ne = remote(
        corner_n, recv_c.at[jnp.where(is_top, 3, 0)], 3,
        jnp.where(is_top, NORTHEAST, SOUTHWEST), ne_lon, north_lat,
    )
    go_nw = remote(
        corner_n, recv_c.at[jnp.where(is_top, 2, 1)], 4,
        jnp.where(is_top, NORTHWEST, SOUTHEAST), nw_lon, north_lat,
    )
    go_s = remote(send_s, recv_ns.at[1], 5, NORTH, lon, lat - 1)
    go_se = remote(corner_s, recv_c.at[2], 6, NORTHWEST, east, lat - 1)
    go_sw = remote(corner_s, recv_c.at[3], 7, NORTHEAST, west, lat - 1)

    def set_coefficients(start):
        piece = pl.ds(start, CHUNK)
        k = scale[piece, :]
        e_weight = weights[0, piece, :]
        n_weight = weights[1, piece, :]
        w_weight = roll(e_weight, 1, 1)
        if start:
            s_weight = weights[1, pl.ds(start - 1, CHUNK), :]
        else:
            s_weight = roll(n_weight, 1, 0)
        ke, kw, kn, ks = k * e_weight, k * w_weight, k * n_weight, k * s_weight
        coef[0, piece, :] = 1.0 - ((ke + kw) + (kn + ks))
        coef[1, piece, :] = ke
        coef[2, piece, :] = kw
        coef[3, piece, :] = kn
        coef[4, piece, :] = ks

    def advance_block():
        for start in starts:
            set_coefficients(start)

        @pl.loop(0, nlevel)
        def _(level):
            def put(field, start, value):
                ext1[field * nlevel + level, pl.ds(PAD + start, CHUNK), :] = value

            advance(ext0, coef, nfield, nlevel, level, put)

        @pl.loop(0, nlevel)
        def _(level):
            def put(field, start, value):
                state[field * nlevel + level, pl.ds(start, CHUNK), :] = value

            advance(ext1, coef, nfield, nlevel, level, put)

        for start in range(0, rows + 2 * PAD, 48):
            piece = pl.ds(start, 48)
            lane = lanes_of((48, LANES))
            gathered = jnp.zeros((48, LANES), jnp.float32)
            for p in range(nplane):
                plane = ext1[p, piece, :]
                gathered = jnp.where(lane // 2 == 2 * p, roll(plane, 4 * p + 3, 1), gathered)
                gathered = jnp.where(lane // 2 == 2 * p + 1, roll(plane, 4 * p + 1, 1), gathered)
            inner[piece, :] = gathered

        for i, row in enumerate((PAD + 1, PAD + 2, top_row - 2, top_row - 3)):
            for p in range(nplane):
                edge_rows[i, pl.ds(p, 1), :] = ext1[p, pl.ds(row, 1), :]

    def gather_rows():
        for buf, first, second, corner in ((send_s, 0, 1, 0), (send_n, rows - 1, rows - 2, rows - 8)):
            for at, row in ((0, first), (28, second)):
                for p in range(nplane):
                    buf[pl.ds(at + p, 1), :] = ext0[p, pl.ds(PAD + row, 1), :]
                for i in range(2):
                    buf[pl.ds(at + nplane + i, 1), :] = weights[i, pl.ds(row, 1), :]
                buf[pl.ds(at + nplane + 2, 1), :] = scale[pl.ds(row, 1), :]
                buf[pl.ds(at + nplane + 3, 1), :] = jnp.zeros((1, LANES), jnp.float32)
            buf[pl.ds(56, 8), :] = packed[pl.ds(corner, 8), :]

    def start_rows():
        go_n.start()

        @pl.when(not_bottom)
        def _():
            go_s.start()

    @pl.when(lon == 0)
    def _():
        advance_block()
        gather_rows()

    greetings = 3 + jnp.where(ne_self, 0, 1) + jnp.where(nw_self, 0, 1) + jnp.where(is_bottom, 0, 3)
    pl.semaphore_wait(barrier, greetings)

    @pl.when(lon == 0)
    def _():
        start_rows()

    @pl.when(ne_other)
    def _():
        go_ne.start()

    @pl.when(nw_other)
    def _():
        go_nw.start()

    @pl.when(not_bottom)
    def _():
        go_se.start()
        go_sw.start()

    go_w.start()
    go_e.start()

    @pl.when(lon != 0)
    def _():
        gather_rows()
        start_rows()

    @pl.when(ne_self)
    def _():
        recv_c[3] = packed[pl.ds(rows - 8, 8), :]

    @pl.when(nw_self)
    def _():
        recv_c[2] = packed[pl.ds(rows - 8, 8), :]

    @pl.when(is_bottom)
    def _():
        recv_ns[0] = jnp.zeros(recv_ns.shape[1:], jnp.float32)
        recv_c[0] = jnp.zeros(recv_c.shape[1:], jnp.float32)
        recv_c[1] = jnp.zeros(recv_c.shape[1:], jnp.float32)

    @pl.when(lon != 0)
    def _():
        advance_block()

    def arrived(dst, slot):
        remote(dst, dst, 0, slot, west, lat).wait_recv()

    arrived(recv_ns.at[1], NORTH)

    @pl.when(not_bottom)
    def _():
        arrived(recv_ns.at[0], SOUTH)

    def at_top(shape):
        return jnp.full(shape, lat, jnp.int32) == nlat - 1

    shape = (56, LANES)
    came = recv_ns[1, pl.ds(0, 56), :]
    sub = rows_of(shape) % 28
    flips = jnp.where(jnp.logical_and(sub >= 4 * nlevel, sub < nplane), -1.0, 1.0)
    nrows[...] = jnp.where(
        at_top(shape), flips * take_lanes(came, LANES - 1 - lanes_of(shape)), came
    )
    srows[...] = recv_ns[0, pl.ds(0, 56), :]

    at_u, at_v = slice(4 * nlevel, 5 * nlevel), slice(5 * nlevel, 6 * nlevel)
    folded_1 = at_top((1, LANES))
    flat = (nplane, LANES)
    lane_f = lanes_of(flat)
    slot_f = lane_f % 4
    column_f = jnp.where(slot_f < 2, LANES - 3 + slot_f, slot_f - 1)

    def spread(value):
        return jnp.concatenate([value] * nfield, axis=0)

    def row_step(x, south, north, k, e_weight, n_south, n_north):
        left, right = roll(x, 1, 1), roll(x, -1, 1)
        ke, kw = k * e_weight, k * roll(e_weight, 1, 1)
        kn, ks = k * n_north, k * n_south
        base = 1.0 - ((ke + kw) + (kn + ks))
        c = coefficients(
            base, ke, kw, kn, ks,
            spread(x[at_u]), spread(left[at_u]), spread(right[at_u]),
            spread(x[at_v]), spread(south[at_v]), spread(north[at_v]),
        )
        return stencil(c, x, left, right, south, north)

    def to_inner(row, value):
        picked = jnp.where(rows_of(flat) == lane_f // 4, take_lanes(value, column_f), 0.0)
        inner[pl.ds(row, 1), :] = jnp.sum(picked, axis=0, keepdims=True)

    def two_rows(buf, first):
        fields_of = buf[pl.ds(first, nplane), :]
        e_weight, n_weight, k = (buf[pl.ds(first + nplane + i, 1), :] for i in range(3))
        return fields_of, k, e_weight, n_weight

    x0, k0, e0, n0 = two_rows(send_s, 0)
    x1, k1, e1, n1 = two_rows(send_s, 28)
    y0, ky, ey, ny = two_rows(srows, 0)
    y1, _, _, ny1 = two_rows(srows, 28)
    out0 = row_step(y0, y1, x0, ky, ey, ny1, ny)
    in0 = row_step(x0, y0, x1, k0, e0, ny, n0)
    in1, in2 = edge_rows[0], edge_rows[1]
    to_inner(low_row, out0)
    to_inner(PAD, in0)
    south_0 = row_step(in0, out0, in1, k0, e0, ny, n0)
    south_1 = row_step(in1, in0, in2, k1, e1, n0, n1)

    x0, k0, e0, n0 = two_rows(send_n, 0)
    x1, k1, e1, n1 = two_rows(send_n, 28)
    n2 = weights[1, pl.ds(rows - 3, 1), :]
    y0, ky, ey, ny = two_rows(nrows, 0)
    y1, _, _, ny1 = two_rows(nrows, 28)
    ey = jnp.where(folded_1, roll(ey, -1, 1), ey)
    out0 = row_step(
        y0, x0, y1, ky, ey, jnp.where(folded_1, ny, n0), jnp.where(folded_1, ny1, ny)
    )
    in0 = row_step(x0, x1, y0, k0, e0, n1, n0)
    in1, in2 = edge_rows[2], edge_rows[3]
    to_inner(top_row, out0)
    to_inner(top_row - 1, in0)
    north_0 = row_step(in0, in1, out0, k0, e0, n1, n0)
    north_1 = row_step(in1, in2, in0, k1, e1, n2, n1)
    for i, value in enumerate((south_0, south_1, north_0, north_1)):
        edge_rows[i] = value
    for i, row in enumerate((0, 1, rows - 1, rows - 2)):
        for p in range(nplane):
            state[p, pl.ds(row, 1), :] = edge_rows[i, pl.ds(p, 1), :]

    eight = (8, LANES)
    lane8 = lanes_of(eight)
    slot8 = lane8 % 4
    flip8 = jnp.where(jnp.logical_and(lane8 >= 16 * nlevel, lane8 < 4 * nplane), -1.0, 1.0)
    east8 = lane8 // 4 == nplane

    def beyond(block):
        upside = jnp.concatenate([block[7 - i : 8 - i, :] for i in range(8)], axis=0)
        mirrored = flip8 * take_lanes(upside, lane8 - slot8 + (3 - slot8))
        mirrored = jnp.where(east8, roll(mirrored, -1, 1), mirrored)
        return mirrored

    tall = (rows + 2 * PAD, LANES)
    slot_t = lanes_of(tall) % 4
    lane_t = lanes_of(tall)
    folded = jnp.logical_and(at_top(tall), rows_of(tall) == top_row)

    beyond_125 = take_lanes(weights[0], jnp.full((rows, LANES), LANES - 3, jnp.int32))
    beyond_125 = jnp.concatenate([beyond_125[:PAD], beyond_125, beyond_125[:PAD]], axis=0)
    inner_all = inner[...]
    index_u = 16 * nlevel + lane_t % (4 * nlevel)
    index_v = 20 * nlevel + lane_t % (4 * nlevel)

    def strip_step(w, x, left, right):
        south, north = roll(x, 1, 0), roll(x, -1, 0)
        u = take_lanes(x, index_u), take_lanes(left, index_u), take_lanes(right, index_u)
        v = take_lanes(x, index_v)
        c = coefficients(*w, *u, v, roll(v, 1, 0), roll(v, -1, 0))
        return stencil(c, x, left, right, south, north)

    middle_n = recv_ns[1, pl.ds(56, 8), :]
    middle_s = recv_ns[0, pl.ds(56, 8), :]
    slot = lane_h % 4
    place = 2 * (lane_h // 4) + lane_h % 2

    for turn in range(2):
        side = jnp.where(lon == 0, 1 - turn, turn)
        corner_other = jnp.where(side == 0, nw_other.astype(jnp.int32), ne_other.astype(jnp.int32))
        arrived(recv_we.at[side], WEST + side)

        @pl.when(not_bottom)
        def _():
            arrived(recv_c.at[side], SOUTHWEST + side)

        @pl.when(corner_other == 1)
        def _():
            arrived(recv_c.at[2 + side], NORTHWEST + side)

        block = recv_we[side]
        for start in (0, half):
            at = place + (64 if start else 0)
            strips[side, pl.ds(PAD + start, half), :] = jnp.where(
                slot // 2 == side, take_lanes(block, at), packed[pl.ds(start, half), :]
            )
        strips[side, pl.ds(0, 8), :] = jnp.where(slot8 // 2 == side, recv_c[side], middle_s)
        corner = recv_c[2 + side]
        strips[side, pl.ds(top_row, 8), :] = jnp.where(
            at_top(eight),
            beyond(jnp.where(slot8 // 2 == 1 - side, corner, middle_n)),
            jnp.where(slot8 // 2 == side, corner, middle_n),
        )
        x = strips[side]
        e_weight, n_weight, k = (
            take_lanes(x, 4 * (nplane + i) + slot_t) for i in range(3)
        )
        w_weight = jnp.where(slot_t == 0, beyond_125, roll(e_weight, 1, 1))
        n_south = jnp.where(folded, n_weight, roll(n_weight, 1, 0))
        n_north = jnp.where(folded, roll(n_weight, -1, 0), n_weight)
        ke, kw, kn, ks = k * e_weight, k * w_weight, k * n_north, k * n_south
        w = (1.0 - ((ke + kw) + (kn + ks)), ke, kw, kn, ks)
        x = strip_step(w, x, roll(x, 1, 1), roll(x, -1, 1))
        x = jnp.where(
            slot_t == 0, roll(inner_all, -1, 1), jnp.where(slot_t == 3, roll(inner_all, 1, 1), x)
        )
        left = jnp.where(slot_t == 0, inner_all, roll(x, 1, 1))
        right = jnp.where(slot_t == 3, inner_all, roll(x, -1, 1))
        strips[side] = strip_step(w, x, left, right)
    final = jnp.where(slot_t < 2, strips[1], strips[0])
    columns[...] = final[PAD : PAD + rows, :]

    go_w.wait_send()
    go_e.wait_send()
    go_n.wait_send()

    @pl.when(ne_other)
    def _():
        go_ne.wait_send()

    @pl.when(nw_other)
    def _():
        go_nw.wait_send()

    @pl.when(not_bottom)
    def _():
        go_s.wait_send()
        go_se.wait_send()
        go_sw.wait_send()


def second_kernel(state, columns, out, obuf, out_sems):
    nplane, rows, cols = state.shape
    lane = lanes_of((rows, cols))
    is_edge = jnp.logical_or(lane < 2, lane >= LANES - 2)
    parts = out_sems.shape[0]
    size = nplane // parts
    copies = []
    for part in range(parts):
        for p in range(part * size, (part + 1) * size):
            obuf[p] = jnp.where(is_edge, roll(columns[...], -(4 * p + 2), 1), state[p])
        piece = pl.ds(part * size, size)
        copies.append(pltpu.make_async_copy(obuf.at[piece], out.at[piece], out_sems.at[part]))
        copies[-1].start()
    for copy in copies:
        copy.wait()


def solution(mesh):
    nlon, nlat = mesh.shape["lon"], mesh.shape["lat"]

    def local(fields, face_weights, inv_area, cell_mask, land_blocks):
        nfield, nlevel, rows, cols = fields.shape
        nplane = nfield * nlevel
        tall = rows + 2 * PAD
        f32 = jnp.float32
        anywhere = pl.BlockSpec(memory_space=pl.ANY)
        near = pl.BlockSpec(memory_space=pltpu.VMEM)

        def far(value):
            return pltpu.with_memory_space_constraint(value, pltpu.HBM)

        def first(*refs):
            first_kernel(nlon, nlat, nfield, nlevel, *refs)

        def second(*refs):
            second_kernel(*refs)

        passed = pl.pallas_call(
            first,
            out_shape=[
                pltpu.VMEM((nplane, rows, cols), f32),
                pltpu.VMEM((rows, cols), f32),
            ],
            in_specs=[anywhere] * 4 + [pl.BlockSpec(memory_space=pltpu.SMEM)],
            out_specs=[near] * 2,
            scratch_shapes=[
                pltpu.VMEM((nplane, tall, cols), f32),
                pltpu.VMEM((nplane, tall, cols), f32),
                pltpu.VMEM((5, rows, cols), f32),
                pltpu.VMEM((2, rows, cols), f32),
                pltpu.VMEM((rows, cols), f32),
                pltpu.VMEM((rows, cols), jnp.int32),
                pltpu.VMEM((rows, cols), f32),
                pltpu.VMEM((rows, cols), f32),
                pltpu.VMEM((64, cols), f32),
                pltpu.VMEM((64, cols), f32),
                pltpu.VMEM((2, rows // 2, cols), f32),
                pltpu.VMEM((2, rows // 2, cols), f32),
                pltpu.VMEM((2, 64, cols), f32),
                pltpu.VMEM((4, 8, cols), f32),
                pltpu.VMEM((tall, cols), f32),
                pltpu.VMEM((2, tall, cols), f32),
                pltpu.VMEM((56, cols), f32),
                pltpu.VMEM((56, cols), f32),
                pltpu.VMEM((4, nplane, cols), f32),
                pltpu.SemaphoreType.DMA((3 + rows // CHUNK,)),
                pltpu.SemaphoreType.DMA((8,)),
                pltpu.SemaphoreType.DMA((8,)),
            ],
            compiler_params=pltpu.CompilerParams(
                collective_id=0, has_side_effects=True, vmem_limit_bytes=16 * 1024 * 1024
            ),
        )(
            far(fields.reshape(nplane, rows, cols)), far(face_weights), far(inv_area),
            far(cell_mask), land_blocks,
        )
        result = pl.pallas_call(
            second,
            out_shape=pltpu.HBM((nplane, rows, cols), f32),
            in_specs=[near] * 2,
            out_specs=anywhere,
            scratch_shapes=[
                pltpu.VMEM((nplane, rows, cols), f32),
                pltpu.SemaphoreType.DMA((8,)),
            ],
            compiler_params=pltpu.CompilerParams(vmem_limit_bytes=16 * 1024 * 1024),
        )(*(pltpu.with_memory_space_constraint(value, pltpu.VMEM) for value in passed))
        return result.reshape(fields.shape)

    in_specs = (
        P(None, None, "lat", "lon"),
        P(None, "lat", "lon"),
        P("lat", "lon"),
        P("lat", "lon"),
        P("lat", "lon"),
    )
    out_specs = P(None, None, "lat", "lon")
    return jax.shard_map(local, mesh=mesh, in_specs=in_specs, out_specs=out_specs, check_vma=False)
```
